32 devices in a mesh: batch: 16 (over z, y, x), seq: 2 (over core).
Axes of the slice: x: 2, y: 2, z: 4, core: 2. Of those that a mesh axis runs over, the one named last changes fastest.
Arguments:
- word_ids: int32 [64, 1024], P('batch', 'seq'), may hold values from 0 to 3839
- buckets: int32 [64], P('batch'), may hold values from 0 to 7
- noise: bfloat16 [64, 1024, 128], P('batch', 'seq'), may hold values from -6 to 6
- table: bfloat16 [3840, 128], P(('batch', 'seq')), may hold values from -10 to 10
- w_in: bfloat16 [128, 768], replicated, may hold values from -0.5 to 0.5
- time_table: float32 [8, 768], replicated, may hold values from -6 to 6
- pos_table: float32 [1024, 768], replicated, may hold values from -6 to 6
- gain_attn: float32 [768], replicated, may hold values from 0.1 to 1.9
- w_qkv: bfloat16 [768, 2304], replicated, may hold values from -0.3125 to 0.3125
- w_out: bfloat16 [768, 768], replicated, may hold values from -0.875 to 0.875
- gain_mlp: float32 [768], replicated, may hold values from 0.1 to 1.9
- w_up: bfloat16 [768, 3072], replicated, may hold values from -0.21875 to 0.21875
- w_down: bfloat16 [3072, 768], replicated, may hold values from -0.109375 to 0.109375
- w_head: bfloat16 [768, 128], replicated, may hold values from -0.21875 to 0.21875
Outputs:
- output: bfloat16 [64, 1024, 768], P('batch', 'seq')
- grad_table: float32 [3840, 128], P(('batch', 'seq'))
- grad_w_in: float32 [128, 768], replicated
- grad_time: float32 [8, 768], replicated
- grad_pos: float32 [1024, 768], replicated
- grad_gain_attn: float32 [768], replicated
- grad_qkv: float32 [768, 2304], replicated
- grad_out: float32 [768, 768], replicated
- grad_gain_mlp: float32 [768], replicated
- grad_up: float32 [768, 3072], replicated
- grad_down: float32 [3072, 768], replicated
- grad_head: float32 [768, 128], replicated
- mean_norm: float32 [], replicated
The draws below stay inside these ranges and needn't reach their ends.
All inputs are finite; a program needn't handle non-finite values.
Results may differ from the reference program's by a relative error of at most 0.0065.
Values may be sent and summed in bfloat16 or wider, within the bound.
No kernel may reach another device: no remote copies, remote signals or barrier semaphores. Data moves between devices by JAX's collectives and lax.ppermute only.
A program may use at most 256 MiB of HBM per device.

```python
import math
import jax
import jax.numpy as jnp
import numpy as np
from jax import lax

D = 768
HEADS = 12
HEAD = 64
FF = 3072
E = 128
LEN = 1024
NB = 8
VOCAB = 3840
SEQS = 64


def draw_table(key, part):
    key = jax.random.fold_in(key, 11)
    row_key, col_key, val_key = jax.random.split(key, 3)
    position = jnp.arange(VOCAB, dtype=jnp.float32) / VOCAB
    row_scale = 10.0 ** position * jnp.exp(jax.random.uniform(row_key, (VOCAB,), minval=-0.3, maxval=0.3))
    entries = jnp.clip(jax.random.normal(val_key, (VOCAB, E)), -6.0, 6.0)
    col_scale = jnp.exp(jax.random.uniform(col_key, (E,), minval=-0.5, maxval=0.5))
    values = entries * row_scale[:, None] * col_scale[None, :] * E ** (-0.5)
    return jnp.clip(values, -9.5, 9.5).astype(jnp.bfloat16)


def set_ends(result, rng, smallest, top_value):
    place = [jax.random.randint(jax.random.fold_in(rng, axis), (), 0, length) for axis, length in enumerate(result.shape)]
    longest = result.shape.index(max(result.shape))
    next_to = place[:longest] + [(place[longest] + 1) % result.shape[longest]] + place[longest + 1:]
    return result.at[tuple(place)].set(smallest).at[tuple(next_to)].set(top_value)


def block_scale(own_key, extent, shards, smallest, high):
    def one(dim, shards_of):
        steps = jax.random.uniform(jax.random.fold_in(jax.random.fold_in(own_key, 6), dim), (shards_of,), jnp.float32, smallest / len(shards), high / len(shards))
        return jnp.repeat(jnp.exp(steps), extent[dim] // shards_of).reshape((-1,) + (1,) * (len(extent) - dim - 1))

    loudness = one(*shards[0])
    for cut in shards[1:]:
        loudness = loudness * one(*cut)
    return loudness


def rank_bounds(amount, skew):
    weights = [(1 << 20) // math.isqrt(standing ** skew) + 1 for standing in range(1, amount + 1)]
    deviation = 1 + sum(weights) // (1 << 30)
    return np.cumsum(np.array([max(1, weight // deviation) for weight in weights]))


def skewed_ids(key, dims, count, lean):
    table = rank_bounds(count, lean)
    ticket = jax.random.randint(jax.random.fold_in(key, 1), dims, 0, int(table[count - 1]))
    grade = jnp.searchsorted(jnp.asarray(table, jnp.int32), ticket, side="right")
    return jax.random.permutation(jax.random.fold_in(key, 2), count)[grade].astype(jnp.int32)


def centred(key, extent, deviation, bound, cuts=(), kind=jnp.bfloat16):
    values = jax.random.normal(key, extent, jnp.float32) * deviation
    if len(cuts) > 0:
        values = block_scale(key, extent, cuts, -0.22, 0.18) * values
    return jnp.clip(values, min=-bound, max=bound).astype(kind)


def setup_inputs(seed: int = 0) -> dict:
    splits = jax.random.split(jax.random.key(seed), 15)
    word_ids = set_ends(skewed_ids(splits[0], (SEQS, LEN), VOCAB, 2), jax.random.fold_in(splits[0], 3), 0, VOCAB - 1).astype(jnp.int32)
    buckets = set_ends(jax.random.randint(splits[1], (SEQS,), 0, NB), jax.random.fold_in(splits[1], 1), 0, NB - 1).astype(jnp.int32)
    noise = centred(splits[2], (SEQS, LEN, E), 1.0, 6.0, ((0, 16), (1, 2)))
    table = draw_table(jax.random.fold_in(splits[14], 71), 0)
    w_in = centred(splits[4], (E, D), E ** -0.5, 0.5)
    time_table = centred(splits[5], (NB, D), 1.0, 6.0, (), jnp.float32)
    pos_table = centred(splits[6], (LEN, D), 1.0, 6.0, (), jnp.float32)
    gain_attn = jnp.clip(1.0 + 0.18 * jax.random.normal(splits[7], (D,), jnp.float32), 0.1, 1.9)
    w_qkv = centred(splits[8], (D, 3 * D), (D // 2) ** -0.5, 0.3125)
    w_out = centred(splits[9], (D, D), (D // 16) ** -0.5, 0.875)
    gain_mlp = jnp.clip(1.0 + 0.18 * jax.random.normal(splits[10], (D,), jnp.float32), 0.1, 1.9)
    w_up = centred(splits[11], (D, FF), D ** -0.5, 0.21875)
    w_down = centred(splits[12], (FF, D), FF ** -0.5, 0.109375)
    w_head = centred(splits[13], (D, E), D ** -0.5, 0.21875)
    return dict(word_ids=word_ids, buckets=buckets, noise=noise, table=table, w_in=w_in, time_table=time_table, pos_table=pos_table, gain_attn=gain_attn, w_qkv=w_qkv, w_out=w_out, gain_mlp=gain_mlp, w_up=w_up, w_down=w_down, w_head=w_head)


@jax.custom_vjp
def low(v):
    return lax.optimization_barrier(v.astype(jnp.bfloat16)).astype(jnp.float32)

@jax.custom_vjp
def low_back(v):
    return v

def low_keep(v):
    return (low(v), None)

def low_pass(kept, grad):
    return (grad,)

def back_keep(v):
    return (v, None)

def back_low(kept, grad):
    return (low(grad),)
low.defvjp(low_keep, low_pass)
low_back.defvjp(back_keep, back_low)

def matmul(left, right):
    return jnp.dot(left, right, precision=lax.Precision.HIGHEST, preferred_element_type=jnp.float32)

def layer_norm(hidden, gain_vec):
    centre = hidden - lax.optimization_barrier(jnp.mean(hidden, axis=-1, keepdims=True))
    return centre * lax.rsqrt(lax.optimization_barrier(jnp.mean(centre * centre, axis=-1, keepdims=True)) + 1e-05) * gain_vec

def attend(packed):
    seq_len = packed.shape[0]
    split_parts = packed.reshape(seq_len, 3, HEADS, HEAD)
    scores = low_back(jnp.einsum('qhd,khd->hqk', split_parts[:, 0], split_parts[:, 1], precision=lax.Precision.HIGHEST) * HEAD ** (-0.5))
    prob_block = jax.nn.softmax(scores, axis=-1)
    mixed_out = jnp.einsum('hqk,khd->qhd', low(prob_block), split_parts[:, 2], precision=lax.Precision.HIGHEST)
    return mixed_out.reshape(seq_len, HEADS * HEAD)

def reference(word_ids, buckets, noise, table, w_in, time_table, pos_table, gain_attn, w_qkv, w_out, gain_mlp, w_up, w_down, w_head):
    bucket_hot = (buckets[:, None] == jnp.arange(NB, dtype=jnp.int32)[None, :]).astype(jnp.float32)
    counts = lax.optimization_barrier(jnp.sum(bucket_hot, axis=0))
    seq_weight = 1.0 / lax.optimization_barrier(jnp.sum(bucket_hot * counts[None, :], axis=1))
    angles = math.pi / 2 * (buckets.astype(jnp.float32) + 1.0) / (NB + 1)
    group_size = math.gcd(SEQS, 4)

    def stack_groups(array):
        return array.reshape((SEQS // group_size, group_size) + array.shape[1:])
    inputs = (stack_groups(word_ids), stack_groups(buckets), stack_groups(noise.astype(jnp.float32)), stack_groups(seq_weight), stack_groups(jnp.cos(angles)), stack_groups(jnp.sin(angles)))
    params = tuple((array.astype(jnp.float32) for array in (table, w_in, time_table, pos_table, gain_attn, w_qkv, w_out, gain_mlp, w_up, w_down, w_head)))

    def forward(table_data, in_data, time_data, pos_data, gain_first, qkv_data, out_data, gain_second, up_data, down_data, head_data):
        row_norms = jnp.sqrt(lax.optimization_barrier(jnp.sum(table_data * table_data, axis=1)) + 1e-06)
        mean_norm = jnp.mean(row_norms)
        factor = math.sqrt(E) / mean_norm

        def one_group(loss_total, item_list):
            id_block, kind_block, fresh_noise, weight_block, sig_block, spread_block = item_list
            clean_emb = table_data[id_block] * factor
            noisy_input = sig_block[:, None, None] * clean_emb + spread_block[:, None, None] * fresh_noise
            stream_in = low_back(matmul(low(noisy_input), in_data)) + time_data[kind_block][:, None, :] + pos_data[None, :, :]
            attn_in = low(layer_norm(stream_in, gain_first))
            packed = low(low_back(matmul(attn_in, qkv_data)))
            mixed_out = low(low_back(lax.map(jax.checkpoint(attend), packed)))
            stream_mid = stream_in + low_back(matmul(mixed_out, out_data))
            mlp_in = low(layer_norm(stream_mid, gain_second))
            up_proj = low_back(matmul(mlp_in, up_data))
            stream_out = stream_mid + low_back(matmul(low(jax.nn.gelu(up_proj)), down_data))
            prediction = low_back(matmul(low(stream_out), head_data))
            mismatch = prediction - clean_emb
            loss_part = jnp.sum(0.5 * lax.optimization_barrier(jnp.sum(mismatch * mismatch, axis=(1, 2))) * weight_block)
            return (loss_total + loss_part, stream_out)
        loss_sum, states = lax.scan(jax.checkpoint(one_group), jnp.zeros((), jnp.float32), inputs)
        return (loss_sum, (states.reshape(SEQS, LEN, D), mean_norm))
    loss_sum, pullback, aux_out = jax.vjp(forward, *params, has_aux=True)
    states, mean_norm = aux_out
    gradients = pullback(jnp.ones_like(loss_sum))
    return (states.astype(jnp.bfloat16), gradients[0], gradients[1], gradients[2], gradients[3], gradients[4], gradients[5], gradients[6], gradients[7], gradients[8], gradients[9], gradients[10], mean_norm)
```

```python
import functools
import math

import jax
import jax.numpy as jnp
from jax import lax
from jax.experimental import pallas as pl
from jax.experimental.pallas import tpu as pltpu
from jax.sharding import PartitionSpec as P

HEAD = 64
BF = jnp.bfloat16
F32 = jnp.float32
NN = (((1,), (0,)), ((), ()))
NT = (((1,), (1,)), ((), ()))
VMEM_BYTES = 60 * 2**20
GELU_A = math.sqrt(2 / math.pi)
GELU_B = 0.044715


def dot(left, right, dims=NN):
    return lax.dot_general(left, right, dims, preferred_element_type=F32)


def params():
    return pltpu.CompilerParams(vmem_limit_bytes=VMEM_BYTES)


def cost(flops, moved, trans=0):
    return pl.CostEstimate(flops=int(flops), bytes_accessed=int(moved), transcendentals=int(trans))


def whole(shape):
    return pl.BlockSpec(shape, lambda *_: (0,) * len(shape), pipeline_mode=pl.Buffered(1))


def smem():
    return pl.BlockSpec(memory_space=pltpu.SMEM)


def normalise(hidden):
    centre = hidden - jnp.mean(hidden, axis=-1, keepdims=True)
    inv = lax.rsqrt(jnp.mean(centre * centre, axis=-1, keepdims=True) + 1e-05)
    return centre * inv, inv


def norm_back(hidden, gain, grad):
    unit, inv = normalise(hidden)
    scaled = grad * gain
    part = inv * (
        scaled
        - jnp.mean(scaled, axis=-1, keepdims=True)
        - unit * jnp.mean(scaled * unit, axis=-1, keepdims=True)
    )
    return part, jnp.sum(grad * unit, axis=0, keepdims=True)


def turned(block):
    return block.astype(F32).T.astype(BF)


def accumulate(ref, first, value):
    @pl.when(first)
    def _():
        ref[...] = value

    @pl.when(jnp.logical_not(first))
    def _():
        ref[...] += value


def embed_kernel(
    scal, ids_ref, table_ref, noise_ref, win_ref, time_ref, pos_ref, gain_ref, wqkv_ref,
    word_ref, noisy_ref, stream_ref, attn_ref, packed_ref, *, tiles, hot,
):
    seq = pl.program_id(0) // tiles
    if hot:
        ids = ids_ref[...]
        rows = table_ref.shape[0]
        step = 1024
        word = None
        for start in range(0, rows, step):
            lane = lax.broadcasted_iota(jnp.int32, (ids.shape[0], step), 1) + start
            one = jnp.where(ids == lane, 1.0, 0.0).astype(BF)
            part = dot(one, table_ref[start : start + step, :])
            word = part if word is None else word + part
        word_ref[...] = word.astype(BF)
    else:
        word = table_ref[...].astype(F32)
        word_ref[...] = table_ref[...]
    clean = word * scal[0, 3]
    noisy = (scal[seq, 0] * clean + scal[seq, 1] * noise_ref[...].astype(F32)).astype(BF)
    noisy_ref[...] = noisy
    stream = dot(noisy, win_ref[...]) + time_ref[pl.ds(seq, 1), :] + pos_ref[...]
    stream_ref[...] = stream
    attn = (normalise(stream)[0] * gain_ref[...]).astype(BF)
    attn_ref[...] = turned(attn)
    packed_ref[...] = dot(attn, wqkv_ref[...]).astype(BF)


def embed(scal, ids, table, noise, w_in, time_rows, pos_table, gain, w_qkv, hot, tm=256):
    tokens, width = noise.shape
    length, model = pos_table.shape
    tiles = length // tm
    wide = w_qkv.shape[1]
    row = lambda cols: pl.BlockSpec((tm, cols), lambda i: (i, 0))
    return pl.pallas_call(
        functools.partial(embed_kernel, tiles=tiles, hot=hot),
        grid=(tokens // tm,),
        in_specs=[
            smem(), pl.BlockSpec((tm, 1), lambda i: (i, 0)),
            whole(table.shape) if hot else row(width), row(width), whole(w_in.shape),
            whole(time_rows.shape), pl.BlockSpec((tm, model), lambda i: (i % tiles, 0)),
            whole(gain.shape), whole(w_qkv.shape),
        ],
        out_specs=[
            row(width), row(width), row(model), pl.BlockSpec((model, tm), lambda i: (0, i)), row(wide),
        ],
        out_shape=[
            jax.ShapeDtypeStruct((tokens, width), BF),
            jax.ShapeDtypeStruct((tokens, width), BF),
            jax.ShapeDtypeStruct((tokens, model), F32),
            jax.ShapeDtypeStruct((model, tokens), BF),
            jax.ShapeDtypeStruct((tokens, wide), BF),
        ],
        compiler_params=params(),
        cost_estimate=cost(2 * tokens * model * (wide + width), 30e6),
        name="embed",
    )(scal, ids, table, noise, w_in, time_rows, pos_table, gain, w_qkv)


def attend_kernel(q_ref, k_ref, v_ref, mixed_ref, probs_ref, inv_ref, *, tq):
    length = q_ref.shape[0]
    lane = lax.broadcasted_iota(jnp.int32, (1, 2 * HEAD), 1)
    keys = k_ref[...]
    values = jnp.concatenate([v_ref[...], jnp.ones_like(v_ref[...])], axis=1)
    scale = math.log2(math.e) * HEAD**-0.5
    for start in range(0, length, tq):
        rows = slice(start, start + tq)
        query = q_ref[rows, :]
        parts = []
        for head in range(2):
            own = jnp.where(lane // HEAD == head, query, jnp.zeros_like(query))
            scores = dot(own, keys, NT)
            peak = jnp.max(scores, axis=1, keepdims=True)
            raised = jnp.exp2(scores * scale - peak * scale).astype(BF)
            probs_ref[head, rows, :] = raised
            sums = dot(raised, values)
            inv = 1.0 / sums[:, 2 * HEAD :]
            parts.append((sums[:, : 2 * HEAD] * inv, inv))
        low = lane < HEAD
        mixed_ref[rows, :] = jnp.where(low, parts[0][0], parts[1][0]).astype(BF)
        inv_ref[rows, :] = jnp.where(low, parts[0][1], parts[1][1])


def attend(packed, length, tq=256):
    tokens = packed.shape[0]
    seqs, pairs = tokens // length, packed.shape[1] // (6 * HEAD)
    spec = lambda part: pl.BlockSpec((length, 2 * HEAD), lambda s, j: (s, part * pairs + j))
    return pl.pallas_call(
        functools.partial(attend_kernel, tq=tq),
        grid=(seqs, pairs),
        in_specs=[spec(0), spec(1), spec(2)],
        out_specs=[
            spec(0), pl.BlockSpec((2, length, length), lambda s, j: (s * pairs + j, 0, 0)), spec(0),
        ],
        out_shape=[
            jax.ShapeDtypeStruct((tokens, pairs * 2 * HEAD), BF),
            jax.ShapeDtypeStruct((seqs * pairs * 2, length, length), BF),
            jax.ShapeDtypeStruct((tokens, pairs * 2 * HEAD), F32),
        ],
        compiler_params=params(),
        cost_estimate=cost(16 * seqs * pairs * length * length * 2 * HEAD, 80e6, 25e6),
        name="attend",
    )(packed, packed, packed)


def attend_back_kernel(
    q_ref, k_ref, v_ref, grad_ref, mixed_ref, inv_ref, probs_ref, dq_ref, dk_ref, dv_ref, *, tq
):
    length = q_ref.shape[0]
    lane = lax.broadcasted_iota(jnp.int32, (1, 2 * HEAD), 1)
    keys, values = k_ref[...], v_ref[...]
    scale = HEAD**-0.5
    held = [None] * (length // tq)
    key_parts, value_parts = [], []
    for head in range(2):
        mask = lane // HEAD == head
        grad_k, grad_v = None, None
        cut = slice(head * HEAD, (head + 1) * HEAD)
        for tile in range(length // tq):
            rows = slice(tile * tq, (tile + 1) * tq)
            grad = grad_ref[rows, :]
            inv = inv_ref[rows, :]
            wide = grad.astype(F32)
            inner = jnp.sum(
                jnp.where(mask, wide * mixed_ref[rows, :].astype(F32), 0.0), axis=1, keepdims=True
            )
            grad_probs = dot(jnp.where(mask, grad, jnp.zeros_like(grad)), values, NT)
            raised = probs_ref[head, rows, :]
            grad_scores = (raised.astype(F32) * (grad_probs - inner)).astype(BF)
            grad_q = dot(grad_scores, keys) * (inv * scale)
            if head == 0:
                held[tile] = grad_q
            else:
                dq_ref[rows, :] = jnp.where(lane < HEAD, held[tile], grad_q).astype(BF)
            query = (q_ref[rows, :].astype(F32) * (inv * scale)).T[cut, :].astype(BF)
            outer = (wide * inv).T[cut, :].astype(BF)
            part_k, part_v = dot(query, grad_scores), dot(outer, raised)
            grad_k = part_k if grad_k is None else grad_k + part_k
            grad_v = part_v if grad_v is None else grad_v + part_v
        key_parts.append(grad_k)
        value_parts.append(grad_v)
    dk_ref[...] = jnp.concatenate(key_parts, axis=0).T.astype(BF)
    dv_ref[...] = jnp.concatenate(value_parts, axis=0).T.astype(BF)


def attend_back(packed, grad_mixed, mixed, inv, probs, length, tq=256):
    tokens = packed.shape[0]
    seqs, pairs = tokens // length, packed.shape[1] // (6 * HEAD)
    spec = lambda part: pl.BlockSpec((length, 2 * HEAD), lambda s, j: (s, part * pairs + j))
    return pl.pallas_call(
        functools.partial(attend_back_kernel, tq=tq),
        grid=(seqs, pairs),
        in_specs=[
            spec(0), spec(1), spec(2), spec(0), spec(0), spec(0),
            pl.BlockSpec((2, length, length), lambda s, j: (s * pairs + j, 0, 0)),
        ],
        out_specs=[spec(0)] * 3,
        out_shape=[jax.ShapeDtypeStruct((tokens, pairs * 2 * HEAD), BF)] * 3,
        compiler_params=params(),
        cost_estimate=cost(32 * seqs * pairs * length * length * 2 * HEAD, 80e6),
        name="attend_back",
    )(packed, packed, packed, grad_mixed, mixed, inv, probs)


def forward_kernel(
    scal, mixed_ref, stream_ref, word_ref, wout_ref, gain_ref, wup_ref, wdown_ref, whead_ref,
    mid_ref, mlp_ref, act_ref, slope_ref, out_ref, gpred_ref, branch_ref, turned_ref, mixed_t_ref,
    ghead_ref,
    *, tiles, step,
):
    index = pl.program_id(0)
    seq = index // tiles
    mid = stream_ref[...] + dot(mixed_ref[...], wout_ref[...])
    mid_ref[...] = mid
    mlp = (normalise(mid)[0] * gain_ref[...]).astype(BF)
    mlp_ref[...] = turned(mlp)
    mixed_t_ref[...] = turned(mixed_ref[...])
    total = mid
    for start in range(0, wup_ref.shape[1], step):
        cols = slice(start, start + step)
        up = dot(mlp, wup_ref[:, cols])
        square = up * up
        bent = jnp.tanh(up * (GELU_A + GELU_A * GELU_B * square))
        half = 0.5 * up
        act = (half + half * bent).astype(BF)
        act_ref[:, cols] = act
        slope = (0.5 + 0.5 * bent) + half * (1.0 - bent * bent) * (
            GELU_A + 3.0 * GELU_A * GELU_B * square
        )
        slope_ref[:, cols] = slope.astype(BF)
        total = total + dot(act, wdown_ref[cols, :])
    low = total.astype(BF)
    out_ref[...] = low
    clean = word_ref[...].astype(F32) * scal[0, 3]
    gpred = (dot(low, whead_ref[...]) - clean) * scal[seq, 2]
    gpred_ref[...] = gpred
    gpred_low = gpred.astype(BF)
    branch = dot(gpred_low, whead_ref[...], NT)
    branch_ref[...] = branch.astype(BF)
    turned_ref[...] = branch.T.astype(BF)
    accumulate(ghead_ref, index == 0, dot(gpred.T.astype(BF), low))


def forward(scal, mixed, stream, word, w_out, gain, w_up, w_down, w_head, length, tm=256, step=768):
    tokens, model = mixed.shape
    inner, width = w_up.shape[1], w_head.shape[1]
    row = lambda cols: pl.BlockSpec((tm, cols), lambda i: (i, 0))
    shape = lambda cols, kind: jax.ShapeDtypeStruct((tokens, cols), kind)
    flip = pl.BlockSpec((model, tm), lambda i: (0, i))
    flipped = jax.ShapeDtypeStruct((model, tokens), BF)
    return pl.pallas_call(
        functools.partial(forward_kernel, tiles=length // tm, step=step),
        grid=(tokens // tm,),
        in_specs=[
            smem(), row(model), row(model), row(width), whole(w_out.shape), whole(gain.shape),
            whole(w_up.shape), whole(w_down.shape), whole(w_head.shape),
        ],
        out_specs=[
            row(model), flip, row(inner), row(inner), row(model), row(width), row(model), flip, flip,
            pl.BlockSpec((width, model), lambda i: (0, 0)),
        ],
        out_shape=[
            shape(model, F32), flipped, shape(inner, BF), shape(inner, BF),
            shape(model, BF), shape(width, F32), shape(model, BF), flipped, flipped,
            jax.ShapeDtypeStruct((width, model), F32),
        ],
        compiler_params=params(),
        cost_estimate=cost(2 * tokens * model * (model + 2 * inner + 3 * width), 60e6),
        name="feed_forward",
    )(scal, mixed, stream, word, w_out, gain, w_up, w_down, w_head)


def back_kernel(
    mid_ref, slope_ref, gpred_ref, branch_ref, wout_ref, gain_ref, wup_ref, wdown_ref, whead_ref,
    upin_ref, gmid_ref, gattn_ref, gmixed_ref, ggain_ref, *, step,
):
    index = pl.program_id(0)
    branch = branch_ref[...]
    grad = None
    for start in range(0, wup_ref.shape[1], step):
        cols = slice(start, start + step)
        upin = (dot(branch, wdown_ref[cols, :], NT) * slope_ref[:, cols].astype(F32)).astype(BF)
        upin_ref[:, cols] = upin
        part = dot(upin, wup_ref[:, cols], NT)
        grad = part if grad is None else grad + part
    part, gain_part = norm_back(mid_ref[...], gain_ref[...], grad)
    accumulate(ggain_ref, index == 0, gain_part)
    gmid = dot(gpred_ref[...].astype(BF), whead_ref[...], NT) + part
    gmid_ref[...] = gmid
    low = gmid.astype(BF)
    gattn_ref[...] = low
    gmixed_ref[...] = dot(low, wout_ref[...], NT).astype(BF)


def back(mid, slope, gpred, branch, w_out, gain, w_up, w_down, w_head, tm=256, step=768):
    tokens, model = mid.shape
    inner, width = w_up.shape[1], w_head.shape[1]
    row = lambda cols: pl.BlockSpec((tm, cols), lambda i: (i, 0))
    shape = lambda cols, kind: jax.ShapeDtypeStruct((tokens, cols), kind)
    return pl.pallas_call(
        functools.partial(back_kernel, step=step),
        grid=(tokens // tm,),
        in_specs=[
            row(model), row(inner), row(width), row(model), whole(w_out.shape), whole(gain.shape),
            whole(w_up.shape), whole(w_down.shape), whole(w_head.shape),
        ],
        out_specs=[
            row(inner), row(model), row(model), row(model),
            pl.BlockSpec((1, model), lambda i: (0, 0)),
        ],
        out_shape=[
            shape(inner, BF), shape(model, F32), shape(model, BF), shape(model, BF),
            jax.ShapeDtypeStruct((1, model), F32),
        ],
        compiler_params=params(),
        cost_estimate=cost(2 * tokens * model * (model + 2 * inner + width), 60e6),
        name="feed_forward_back",
    )(mid, slope, gpred, branch, w_out, gain, w_up, w_down, w_head)


def input_back_kernel(
    scal, gmid_ref, dq_ref, dk_ref, dv_ref, stream_ref, noisy_ref, word_ref, gpred_ref, gain_ref,
    wqkv_ref, win_ref, gpos_ref, gtime_ref, ggain_ref, gwin_ref, grows_ref, gscale_ref,
):
    tile, seq = pl.program_id(0), pl.program_id(1)
    first = jnp.logical_and(tile == 0, seq == 0)
    model = win_ref.shape[1]
    grad = (
        dot(dq_ref[...], wqkv_ref[:, :model], NT)
        + dot(dk_ref[...], wqkv_ref[:, model : 2 * model], NT)
        + dot(dv_ref[...], wqkv_ref[:, 2 * model :], NT)
    )
    part, gain_part = norm_back(stream_ref[...], gain_ref[...], grad)
    accumulate(ggain_ref, first, gain_part)
    gin = gmid_ref[...] + part
    accumulate(gpos_ref, seq == 0, gin)
    sums = jnp.sum(gin, axis=0, keepdims=True)
    @pl.when(tile == 0)
    def _():
        gtime_ref[pl.ds(seq, 1), :] = sums

    @pl.when(tile > 0)
    def _():
        gtime_ref[pl.ds(seq, 1), :] += sums

    low = gin.astype(BF)
    accumulate(gwin_ref, first, dot(noisy_ref[...].astype(F32).T.astype(BF), low))
    gclean = scal[seq, 0] * dot(low, win_ref[...], NT) - gpred_ref[...]
    grows_ref[...] = (gclean * scal[0, 3]).astype(BF)
    accumulate(
        gscale_ref, first, jnp.sum(word_ref[...].astype(F32) * gclean, axis=0, keepdims=True)
    )


def input_back(scal, gmid, dq, dk, dv, stream, noisy, word, gpred, gain, w_qkv, w_in, length, tm=256):
    tokens, model = gmid.shape
    width = w_in.shape[0]
    seqs, tiles = tokens // length, length // tm
    row = lambda cols: pl.BlockSpec((tm, cols), lambda i, s: (s * tiles + i, 0))
    fixed = lambda rows, cols: pl.BlockSpec((rows, cols), lambda i, s: (0, 0))
    return pl.pallas_call(
        input_back_kernel,
        grid=(tiles, seqs),
        in_specs=[
            smem(), row(model), row(model), row(model), row(model), row(model), row(width),
            row(width), row(width), whole(gain.shape), whole(w_qkv.shape), whole(w_in.shape),
        ],
        out_specs=[
            pl.BlockSpec((tm, model), lambda i, s: (i, 0)), fixed(seqs, model), fixed(1, model),
            fixed(width, model), row(width), fixed(1, width),
        ],
        out_shape=[
            jax.ShapeDtypeStruct((length, model), F32),
            jax.ShapeDtypeStruct((seqs, model), F32),
            jax.ShapeDtypeStruct((1, model), F32),
            jax.ShapeDtypeStruct((width, model), F32),
            jax.ShapeDtypeStruct((tokens, width), BF),
            jax.ShapeDtypeStruct((1, width), F32),
        ],
        compiler_params=params(),
        cost_estimate=cost(2 * tokens * model * (3 * model + 2 * width), 30e6),
        name="input_back",
    )(scal, gmid, dq, dk, dv, stream, noisy, word, gpred, gain, w_qkv, w_in)


def rows_kernel(ids_ref, grows_ref, out_ref, *, tv):
    start = pl.program_id(0) * tv
    row = lax.broadcasted_iota(jnp.int32, (tv, ids_ref.shape[1]), 0) + start
    one = jnp.where(row == ids_ref[...], 1.0, 0.0).astype(BF)
    out_ref[...] = dot(one, grows_ref[...])


def table_rows(ids, grows, rows, tv=512):
    tokens, width = grows.shape
    return pl.pallas_call(
        functools.partial(rows_kernel, tv=tv),
        grid=(rows // tv,),
        in_specs=[whole((1, tokens)), whole(grows.shape)],
        out_specs=pl.BlockSpec((tv, width), lambda i: (i, 0)),
        out_shape=jax.ShapeDtypeStruct((rows, width), F32),
        compiler_params=params(),
        cost_estimate=cost(4 * tokens * rows * width, 3e6),
        name="table_rows",
    )(ids, grows)


def bit_orders(batch):
    bits = list(range(batch.bit_length() - 1))
    other = bits[1::-1] + bits[2:] if len(bits) > 1 else bits
    return bits, other


def place(owner, me, order):
    apart = jnp.bitwise_xor(owner, me)
    spot = 0
    for bit in order:
        spot = spot * 2 + jnp.bitwise_and(lax.shift_right_logical(apart, bit), 1)
    return spot


def outer_kernel(where, left_ref, right_ref, out_ref, *, tw, orders, send, row_blocks):
    me, core = where[0], where[1]
    half = 1 - core if send else core
    chunks, rows, cols = out_ref.shape
    col_blocks = chunks // row_blocks
    step = pl.program_id(0)
    acc = dot(left_ref[...], right_ref[...])
    per = cols // tw
    block = step // per
    offset = pl.multiple_of((step % per) * tw, 128)
    for index in range(row_blocks):
        owner = index * col_blocks + block
        spot = jnp.where(half == 0, place(owner, me, orders[0]), place(owner, me, orders[1]))
        out_ref[spot, :, pl.ds(offset, tw)] = acc[index * rows : (index + 1) * rows, :].astype(
            out_ref.dtype
        )


def chunk_shape(batch, rows, cols):
    row_blocks = min(batch, 16 if batch <= 16 else 32)
    return row_blocks, rows // row_blocks, cols * row_blocks // batch


def outer(where, left, right, batch, send, tw=768):
    rows, tokens = left.shape
    half_cols = right.shape[1] // 2
    row_blocks, chunk_rows, chunk_cols = chunk_shape(batch, rows, half_cols)
    tw = min(tw, chunk_cols)
    steps = half_cols // tw
    pick = (lambda i, w: (0, (1 - w[1]) * steps + i)) if send else (lambda i, w: (0, w[1] * steps + i))
    return pl.pallas_call(
        functools.partial(
            outer_kernel, tw=tw, orders=bit_orders(batch), send=send, row_blocks=row_blocks
        ),
        grid_spec=pltpu.PrefetchScalarGridSpec(
            num_scalar_prefetch=1,
            grid=(steps,),
            in_specs=[whole(left.shape), pl.BlockSpec((tokens, tw), pick)],
            out_specs=pl.BlockSpec((batch, chunk_rows, chunk_cols), lambda i, w: (0, 0, 0)),
        ),
        out_shape=jax.ShapeDtypeStruct((batch, chunk_rows, chunk_cols), BF if send else F32),
        compiler_params=params(),
        cost_estimate=cost(2 * tokens * rows * half_cols, 14e6),
        name="weight_grad_send" if send else "weight_grad_keep",
    )(where, left, right)


def outer_attn_kernel(where, attn_ref, mixed_ref, *refs, orders, row_blocks):
    rights, keep_ref, send_ref = refs[:4], refs[4], refs[5]
    me, core = where[0], where[1]
    chunks, rows, cols = keep_ref.shape
    col_blocks = chunks // row_blocks
    model = attn_ref.shape[0]
    tw = min(cols, model)
    for part in range(4):
        half = part // 2
        left_ref = mixed_ref if part == 3 else attn_ref
        for start in range(0, model, tw):
            acc = dot(left_ref[...], rights[part][:, start : start + tw])
            place_at = (part % 2) * model + start
            block, offset = place_at // cols, place_at % cols

            def write(ref):
                for index in range(row_blocks):
                    spot = place(index * col_blocks + block, me, orders[half])
                    ref[spot, :, offset : offset + tw] = acc[
                        index * rows : (index + 1) * rows, :
                    ].astype(ref.dtype)

            @pl.when(core == half)
            def _():
                write(keep_ref)

            @pl.when(core != half)
            def _():
                write(send_ref)


def outer_attn(where, attn, mixed, dq, dk, dv, gattn, batch):
    model, tokens = attn.shape
    row_blocks, chunk_rows, chunk_cols = chunk_shape(batch, model, 2 * model)
    shape = (batch, chunk_rows, chunk_cols)
    return pl.pallas_call(
        functools.partial(outer_attn_kernel, orders=bit_orders(batch), row_blocks=row_blocks),
        grid_spec=pltpu.PrefetchScalarGridSpec(
            num_scalar_prefetch=1,
            grid=(1,),
            in_specs=[whole(attn.shape)] * 2 + [whole(dq.shape)] * 4,
            out_specs=[whole(shape)] * 2,
        ),
        out_shape=[jax.ShapeDtypeStruct(shape, F32), jax.ShapeDtypeStruct(shape, BF)],
        compiler_params=params(),
        cost_estimate=cost(8 * tokens * model * model, 30e6),
        name="attn_weight_grad",
    )(where, attn, mixed, dq, dk, dv, gattn)


def swap(array):
    return lax.ppermute(array, "seq", [(0, 1), (1, 0)])


def hop(array, step):
    batch = lax.axis_size("batch")
    orders = bit_orders(batch)
    pairs = [
        (2 * me + core, 2 * (me ^ (1 << orders[core][step])) + core)
        for me in range(batch)
        for core in range(2)
    ]
    return lax.ppermute(array, ("batch", "seq"), pairs)


def reduce_chunks(keep, send):
    got = swap(send)
    for step in range(lax.axis_size("batch").bit_length() - 1):
        count = keep.shape[0] // 2
        low = (keep[count:] + got[count:].astype(F32)).astype(BF)
        keep = keep[:count] + got[:count].astype(F32)
        got = hop(low, step)
    return keep[0] + got[0].astype(F32)


def share(chunk):
    return lax.all_gather(chunk.astype(BF), ("batch", "seq"), axis=0)


def spread_kernel(in_ref, out_ref, *, flip):
    row_blocks, _, _, rows, cols = in_ref.shape
    whole_rows = in_ref[...].reshape(row_blocks * rows, cols).astype(F32)
    out_ref[...] = whole_rows.T if flip else whole_rows


def spread(gathered, batch, rows, cols, first=0, last=None, flip=False, tw=256):
    last = cols if last is None else last
    row_blocks, chunk_rows, chunk_cols = chunk_shape(batch, rows, cols // 2)
    view = gathered.reshape(row_blocks, batch // row_blocks, 2, chunk_rows, chunk_cols)
    per = chunk_cols // tw if chunk_cols % tw == 0 else 0
    if not per:
        tw = 128
        per = chunk_cols // tw
    half = cols // 2 // tw

    def pick(i):
        at = i + first // tw
        return (0, (at % half) // per, at // half, 0, at % per)

    shape = (last - first, rows) if flip else (rows, last - first)
    return pl.pallas_call(
        functools.partial(spread_kernel, flip=flip),
        grid=((last - first) // tw,),
        in_specs=[pl.BlockSpec((row_blocks, 1, 1, chunk_rows, tw), pick)],
        out_specs=pl.BlockSpec((tw, rows), lambda i: (i, 0))
        if flip
        else pl.BlockSpec((rows, tw), lambda i: (0, i)),
        out_shape=jax.ShapeDtypeStruct(shape, F32),
        compiler_params=params(),
        cost_estimate=cost(0, 6 * rows * (last - first)),
        name="spread",
    )(view)


def small_plan(rows, devices):
    each = -(-sum(rows) // devices // 16) * 16
    plan = [[] for _ in range(devices)]
    start = 0
    for source, count in enumerate(rows):
        done = 0
        while done < count:
            chunk, at = divmod(start + done, each)
            size = min(count - done, each - at)
            plan[chunk].append((source, done, at, size))
            done += size
        start += count
    return each, plan


def pack_kernel(where, *refs, each, plan, orders, span):
    sources, table_ref, keep_ref, send_ref = refs[:-3], refs[-3], refs[-2], refs[-1]
    me, core = where[0], where[1]
    batch = keep_ref.shape[0]
    panels = sources[0].shape[1] // 128
    for chunk, pieces in enumerate(plan):
        half, owner = divmod(chunk, batch)
        spot = place(owner, me, orders[half])

        def write(ref):
            for panel in range(panels):
                base = panel * each
                filled = 0
                for source, first, at, size in pieces:
                    ref[spot, base + at : base + at + size, :] = sources[source][
                        first : first + size, panel * 128 : (panel + 1) * 128
                    ].astype(ref.dtype)
                    filled = at + size
                if filled < each:
                    ref[spot, base + filled : base + each, :] = jnp.zeros(
                        (each - filled, 128), ref.dtype
                    )
            at = (owner * 2 + half) * span
            ref[spot, panels * each :, :] = table_ref[at : at + span, :].astype(ref.dtype)

        @pl.when(core == half)
        def _():
            write(keep_ref)

        @pl.when(core != half)
        def _():
            write(send_ref)


def pack(where, sources, table, batch):
    devices = 2 * batch
    each, plan = small_plan([source.shape[0] for source in sources], devices)
    span = table.shape[0] // devices
    shape = (batch, each * (sources[0].shape[1] // 128) + span, 128)
    return pl.pallas_call(
        functools.partial(pack_kernel, each=each, plan=plan, orders=bit_orders(batch), span=span),
        grid_spec=pltpu.PrefetchScalarGridSpec(
            num_scalar_prefetch=1,
            grid=(1,),
            in_specs=[whole(source.shape) for source in sources] + [whole(table.shape)],
            out_specs=[whole(shape)] * 2,
        ),
        out_shape=[jax.ShapeDtypeStruct(shape, F32), jax.ShapeDtypeStruct(shape, BF)],
        compiler_params=params(),
        cost_estimate=cost(0, 15e6),
        name="pack_small",
    )(where, *sources, table)


def unpack_kernel(in_ref, *outs, each, plan, batch):
    panels = outs[0].shape[1] // 128
    for chunk, pieces in enumerate(plan):
        half, owner = divmod(chunk, batch)
        for panel in range(panels):
            for source, first, at, size in pieces:
                base = panel * each + at
                outs[source][first : first + size, panel * 128 : (panel + 1) * 128] = in_ref[
                    owner * 2 + half, base : base + size, :
                ].astype(F32)


def unpack(gathered, shapes):
    devices = gathered.shape[0]
    each, plan = small_plan([shape[0] for shape in shapes], devices)
    return pl.pallas_call(
        functools.partial(unpack_kernel, each=each, plan=plan, batch=devices // 2),
        grid=(1,),
        in_specs=[whole(gathered.shape)],
        out_specs=[whole(shape) for shape in shapes],
        out_shape=[jax.ShapeDtypeStruct(shape, F32) for shape in shapes],
        compiler_params=params(),
        cost_estimate=cost(0, 8e6),
        name="unpack_small",
    )(gathered)


def local(
    word_ids, buckets, noise, table, w_in, time_table, pos_table, gain_attn, w_qkv, w_out,
    gain_mlp, w_up, w_down, w_head,
):
    seq_rows, half_len = word_ids.shape
    table_span, embed_width = table.shape
    model = w_qkv.shape[0]
    bucket_count = time_table.shape[0]
    batch, cores = lax.axis_size("batch"), lax.axis_size("seq")
    devices = batch * cores
    vocab = table_span * devices
    length = half_len * cores
    seqs = seq_rows // cores
    tokens = seqs * length
    me = lax.axis_index("batch").astype(jnp.int32)
    core = lax.axis_index("seq").astype(jnp.int32)
    where = jnp.stack([me, core])

    def regroup(array):
        own = lax.dynamic_slice_in_dim(array, core * seqs, seqs, 0)
        other = swap(lax.dynamic_slice_in_dim(array, (1 - core) * seqs, seqs, 0))
        return jnp.concatenate(
            [jnp.where(core == 0, own, other), jnp.where(core == 0, other, own)], axis=1
        )

    bucket_hot = (buckets[:, None] == jnp.arange(bucket_count, dtype=jnp.int32)[None, :]).astype(F32)
    span = -(-(table_span + 1) // 16) * 16
    extra = jnp.zeros((span - table_span, embed_width), BF)
    extra = lax.dynamic_update_slice(extra, jnp.sum(bucket_hot, axis=0).astype(BF)[None, :], (0, 0))
    gathered = lax.all_gather(
        jnp.concatenate([table, extra], axis=0), ("batch", "seq"), axis=0
    )
    ids = regroup(word_ids).reshape(tokens, 1)
    ids = (ids // table_span) * span + ids % table_span
    noise_rows = regroup(noise).reshape(tokens, embed_width)
    counts = jnp.sum(gathered[:, table_span, :bucket_count].astype(F32), axis=0) / cores
    body = gathered[:, :table_span, :].astype(F32)
    mean_norm = jnp.sum(jnp.sqrt(jnp.sum(body * body, axis=2) + 1e-06)) / vocab
    factor = math.sqrt(embed_width) / mean_norm

    own_buckets = lax.dynamic_slice_in_dim(buckets, core * seqs, seqs, 0)
    own_hot = (own_buckets[:, None] == jnp.arange(bucket_count, dtype=jnp.int32)[None, :]).astype(F32)
    angles = math.pi / 2 * (own_buckets.astype(F32) + 1.0) / (bucket_count + 1)
    weight = 1.0 / jnp.sum(own_hot * counts[None, :], axis=1)
    scal = jnp.stack(
        [jnp.cos(angles), jnp.sin(angles), weight, jnp.broadcast_to(factor, (seqs,))], axis=1
    )
    time_rows = jnp.dot(own_hot, time_table, precision=lax.Precision.HIGHEST)

    flat_table = gathered.reshape(devices * span, embed_width)
    hot = devices * span <= 8192
    words = flat_table if hot else jnp.take(flat_table, ids[:, 0], axis=0)
    gain_a, gain_m = gain_attn.reshape(1, model), gain_mlp.reshape(1, model)
    word, noisy, stream, attn_t, packed = embed(
        scal, ids, words, noise_rows, w_in, time_rows, pos_table, gain_a, w_qkv, hot
    )
    mixed, probs, inv = attend(packed, length)
    mid, mlp_t, act, slope, low, gpred, branch, branch_t, mixed_t, ghead = forward(
        scal, mixed, stream, word, w_out, gain_m, w_up, w_down, w_head, length
    )
    down_send = outer(where, branch_t, act, batch, True)
    down_keep = outer(where, branch_t, act, batch, False)
    upin, gmid, gattn, gmixed, ggain_m = back(
        mid, slope, gpred, branch, w_out, gain_m, w_up, w_down, w_head
    )
    up_send = outer(where, mlp_t, upin, batch, True)
    up_keep = outer(where, mlp_t, upin, batch, False)
    dq, dk, dv = attend_back(packed, gmixed, mixed, inv, probs, length)
    attn_keep, attn_send = outer_attn(where, attn_t, mixed_t, dq, dk, dv, gattn, batch)
    gpos, gtime, ggain_a, gwin, grows, gscale = input_back(
        scal, gmid, dq, dk, dv, stream, noisy, word, gpred, gain_a, w_qkv, w_in, length
    )
    rows = table_rows(ids.reshape(1, tokens), grows, devices * span)

    down_all = share(reduce_chunks(down_keep, down_send))
    up_all = share(reduce_chunks(up_keep, up_send))
    attn_all = share(reduce_chunks(attn_keep, attn_send))
    grad_time = jnp.dot(own_hot.T, gtime, precision=lax.Precision.HIGHEST)
    extras = jnp.concatenate(
        [
            grad_time, ggain_a, ggain_m,
            jnp.pad(jnp.sum(gscale).reshape(1, 1), ((0, 0), (0, model - 1))),
            jnp.zeros((16 - bucket_count - 3, model), F32),
        ],
        axis=0,
    )
    small = [gpos, gwin, ghead, extras]
    keep, send = pack(where, small, rows, batch)
    mine = reduce_chunks(keep, send)
    cut = mine.shape[0] - span
    pos_sum, win_sum, head_sum, extra_sum = unpack(share(mine[:cut]), [a.shape for a in small])

    table_data = table.astype(F32)
    own_norms = jnp.sqrt(jnp.sum(table_data * table_data, axis=1, keepdims=True) + 1e-06)
    grad_mean = -math.sqrt(embed_width) / (mean_norm * mean_norm) * extra_sum[bucket_count + 2, 0]
    grad_table = mine[cut : cut + table_span] + grad_mean / vocab * table_data / own_norms

    low = low.reshape(seqs, length, model)
    own = lax.dynamic_slice_in_dim(low, core * half_len, half_len, 1)
    other = swap(lax.dynamic_slice_in_dim(low, (1 - core) * half_len, half_len, 1))
    output = jnp.concatenate(
        [jnp.where(core == 0, own, other), jnp.where(core == 0, other, own)], axis=0
    )
    inner = w_up.shape[1]
    return (
        output,
        grad_table,
        win_sum,
        extra_sum[:bucket_count],
        pos_sum,
        extra_sum[bucket_count],
        spread(attn_all, batch, model, 4 * model, 0, 3 * model),
        spread(attn_all, batch, model, 4 * model, 3 * model, 4 * model),
        extra_sum[bucket_count + 1],
        spread(up_all, batch, model, inner),
        spread(down_all, batch, model, inner, flip=True),
        head_sum.T,
        mean_norm,
    )


def solution(mesh):
    rows = P(("batch", "seq"), None)
    in_specs = (P("batch", "seq"), P("batch"), P("batch", "seq", None), rows) + (P(),) * 10
    out_specs = (P("batch", "seq", None), rows) + (P(),) * 11
    return jax.shard_map(local, mesh=mesh, in_specs=in_specs, out_specs=out_specs, check_vma=False)
```

```python
import functools
import math

import jax
import jax.numpy as jnp
from jax import lax
from jax.experimental import pallas as pl
from jax.experimental.pallas import tpu as pltpu
from jax.sharding import PartitionSpec as P

HEAD = 64
BF = jnp.bfloat16
F32 = jnp.float32
NN = (((1,), (0,)), ((), ()))
NT = (((1,), (1,)), ((), ()))
TN = (((0,), (0,)), ((), ()))
VMEM_BYTES = 60 * 2**20
GELU_A = math.sqrt(2 / math.pi)
GELU_B = 0.044715


def dot(left, right, dims=NN):
    return lax.dot_general(left, right, dims, preferred_element_type=F32)


def params(limit=VMEM_BYTES):
    return pltpu.CompilerParams(vmem_limit_bytes=limit)


def cost(micros):
    return pl.CostEstimate(flops=int(micros * 1.2e9), bytes_accessed=0, transcendentals=0)


def whole(shape):
    return pl.BlockSpec(shape, lambda *_: (0,) * len(shape), pipeline_mode=pl.Buffered(1))


def smem():
    return pl.BlockSpec(memory_space=pltpu.SMEM)


def normalise(hidden):
    centre = hidden - jnp.mean(hidden, axis=-1, keepdims=True)
    inv = lax.rsqrt(jnp.mean(centre * centre, axis=-1, keepdims=True) + 1e-05)
    return centre * inv, inv


def norm_back(hidden, gain, grad):
    unit, inv = normalise(hidden)
    scaled = grad * gain
    part = inv * (
        scaled
        - jnp.mean(scaled, axis=-1, keepdims=True)
        - unit * jnp.mean(scaled * unit, axis=-1, keepdims=True)
    )
    return part, jnp.sum(grad * unit, axis=0, keepdims=True)


ORDER = []


def launch(kernel, inputs, in_specs, out_specs, out_shape, grid, name, estimate, prefetch=(), aliases=None, scratch=(), limit=VMEM_BYTES, chained=True):
    count = len(prefetch) + len(inputs)
    outs, waits = len(out_shape), len(ORDER)

    def body(*refs):
        at = count + waits
        refs[at + outs][...] = jnp.zeros((8, 128), F32)
        kernel(*refs[:count], *refs[at : at + outs], *refs[at + outs + 1 :])

    token = pl.BlockSpec((8, 128), lambda *_: (0, 0))
    *results, last = pl.pallas_call(
        body,
        grid_spec=pltpu.PrefetchScalarGridSpec(
            num_scalar_prefetch=len(prefetch),
            grid=grid,
            in_specs=list(in_specs) + [whole((8, 128))] * waits,
            out_specs=list(out_specs) + [token],
            scratch_shapes=list(scratch),
        ),
        out_shape=list(out_shape) + [jax.ShapeDtypeStruct((8, 128), F32)],
        input_output_aliases={len(prefetch) + k: v for k, v in (aliases or {}).items()},
        compiler_params=params(limit),
        cost_estimate=estimate,
        name=name,
    )(*prefetch, *inputs, *ORDER)
    if chained:
        ORDER[:] = [last]
    return results


def anywhere(count):
    return [pl.BlockSpec(memory_space=pl.ANY)] * count


def ignoring(kernel, inputs, extra):
    return lambda *refs: kernel(*refs[:inputs], *refs[inputs + extra :])


def accumulate(ref, first, value):
    @pl.when(first)
    def _():
        ref[...] = value

    @pl.when(jnp.logical_not(first))
    def _():
        ref[...] += value


def embed_kernel(
    buckets, ids_ref, own_ref, other_ref, noise_ref, win_ref, time_ref, pos_ref, gain_ref, wqkv_ref,
    word_ref, noisy_ref, stream_ref, left_ref, packed_ref, scal_ref, table_ref,
    *, tiles, table_span, seqs, step,
):
    index = pl.program_id(0)
    seq = index // tiles
    chunks, span, width = own_ref.shape
    bucket_count = time_ref.shape[0]

    @pl.when(index == 0)
    def _():
        real = lax.broadcasted_iota(jnp.int32, (span, 1), 0) < table_span
        norms = jnp.zeros((span, 1), F32)
        counts = jnp.zeros((1, width), F32)
        for half, ref in enumerate((own_ref, other_ref)):
            for chunk in range(chunks):
                block = ref[chunk].astype(F32)
                norms += jnp.where(
                    real, jnp.sqrt(jnp.sum(block * block, axis=1, keepdims=True) + 1e-06), 0.0
                )
                counts += block[table_span : table_span + 1, :]
                at = (half * chunks + chunk) * span
                table_ref[:, at : at + span] = block.T.astype(BF)
        mean_norm = jnp.sum(norms, axis=0, keepdims=True) / (2 * chunks * table_span)
        lane = lax.broadcasted_iota(jnp.int32, (1, width), 1)
        scal_ref[...] = jnp.zeros_like(scal_ref)
        for each in range(seqs):
            bucket = buckets[each]
            signal, spread = jnp.float32(0.0), jnp.float32(0.0)
            for kind in range(bucket_count):
                angle = math.pi / 2 * (kind + 1.0) / (bucket_count + 1)
                signal = jnp.where(bucket == kind, math.cos(angle), signal)
                spread = jnp.where(bucket == kind, math.sin(angle), spread)
            count = jnp.sum(jnp.where(lane == bucket, counts, 0.0), axis=1, keepdims=True)
            row = jnp.where(lane == 0, signal, jnp.where(lane == 1, spread, 0.0))
            row = jnp.where(lane == 2, 2.0 / count, row)
            row = jnp.where(lane == 3, math.sqrt(width) / mean_norm, row)
            scal_ref[each : each + 1, :] = jnp.where(lane == 4, mean_norm, row)

    ids = ids_ref[...]
    word = jnp.zeros((width, ids.shape[1]), F32)
    for start in range(0, 2 * chunks * span, step):
        row = lax.broadcasted_iota(jnp.int32, (step, ids.shape[1]), 0) + start
        one = jnp.where(row == ids, 1.0, 0.0).astype(BF)
        word += dot(table_ref[:, start : start + step], one)
    word = word.T
    word_ref[...] = word.astype(BF)
    scal = scal_ref[pl.ds(seq, 1), :]
    clean = word * scal[:, 3:4]
    noisy = (scal[:, 0:1] * clean + scal[:, 1:2] * noise_ref[...].astype(F32)).astype(BF)
    noisy_ref[...] = noisy
    stream = dot(noisy, win_ref[...]) + time_ref[pl.ds(buckets[seq], 1), :] + pos_ref[...]
    stream_ref[...] = stream
    attn = (normalise(stream)[0] * gain_ref[...]).astype(BF)
    left_ref[0] = attn
    packed_ref[...] = dot(attn, wqkv_ref[...]).astype(BF)


def embed(buckets, ids, own, other, noise, w_in, time_table, pos_table, gain, w_qkv, table_span, tm=256):
    tokens, width = noise.shape
    length, model = pos_table.shape
    seqs, tiles = tokens // length, length // tm
    wide = w_qkv.shape[1]
    rows = 2 * own.shape[0] * own.shape[1]
    row = lambda cols: pl.BlockSpec((tm, cols), lambda i: (i, 0))
    return launch(
        functools.partial(
            embed_kernel, tiles=tiles, table_span=table_span, seqs=seqs, step=min(rows, 1024)
        ),
        [buckets, ids, own, other, noise, w_in, time_table, pos_table, gain, w_qkv],
        [
            smem(), pl.BlockSpec((1, tm), lambda i: (0, i)), whole(own.shape), whole(other.shape),
            row(width), whole(w_in.shape), whole(time_table.shape),
            pl.BlockSpec((tm, model), lambda i: (i % tiles, 0)), whole(gain.shape), whole(w_qkv.shape),
        ],
        [
            row(width), row(width), row(model), pl.BlockSpec((1, tm, model), lambda i: (0, i, 0)),
            row(wide), pl.BlockSpec((8, width), lambda i: (0, 0)),
        ],
        [
            jax.ShapeDtypeStruct((tokens, width), BF),
            jax.ShapeDtypeStruct((tokens, width), BF),
            jax.ShapeDtypeStruct((tokens, model), F32),
            jax.ShapeDtypeStruct((2, tokens, model), BF),
            jax.ShapeDtypeStruct((tokens, wide), BF),
            jax.ShapeDtypeStruct((8, width), F32),
        ],
        (tokens // tm,),
        "embed",
        cost(tokens / 80),
        scratch=[pltpu.VMEM((width, rows), BF)],
    )


def attend_kernel(q_ref, k_ref, v_ref, mixed_ref, probs_ref, inv_ref, *, tq):
    length = q_ref.shape[0]
    lane = lax.broadcasted_iota(jnp.int32, (1, 2 * HEAD), 1)
    keys = k_ref[...]
    values = jnp.concatenate([v_ref[...], jnp.ones_like(v_ref[...])], axis=1)
    scale = math.log2(math.e) * HEAD**-0.5
    for start in range(0, length, tq):
        rows = slice(start, start + tq)
        query = q_ref[rows, :]
        parts = []
        for head in range(2):
            own = jnp.where(lane // HEAD == head, query, jnp.zeros_like(query))
            scores = dot(own, keys, NT)
            peak = jnp.max(scores, axis=1, keepdims=True)
            raised = jnp.exp2(scores * scale - peak * scale).astype(BF)
            probs_ref[head, rows, :] = raised
            sums = dot(raised, values)
            inv = 1.0 / sums[:, 2 * HEAD :]
            parts.append((sums[:, : 2 * HEAD] * inv, inv))
        low = lane < HEAD
        mixed_ref[0, rows, :] = jnp.where(low, parts[0][0], parts[1][0]).astype(BF)
        inv_ref[rows, :] = jnp.where(low, parts[0][1], parts[1][1])


def attend(packed, length, lefts, tq=256):
    tokens = packed.shape[0]
    seqs, pairs = tokens // length, packed.shape[1] // (6 * HEAD)
    spec = lambda part: pl.BlockSpec((length, 2 * HEAD), lambda s, j: (s, part * pairs + j))
    return launch(
        ignoring(functools.partial(attend_kernel, tq=tq), 3, 1),
        [packed, packed, packed, lefts],
        [spec(0), spec(1), spec(2)] + anywhere(1),
        [
            pl.BlockSpec((1, length, 2 * HEAD), lambda s, j: (1, s, j)),
            pl.BlockSpec((2, length, length), lambda s, j: (s * pairs + j, 0, 0)), spec(0),
        ],
        [
            jax.ShapeDtypeStruct(lefts.shape, BF),
            jax.ShapeDtypeStruct((seqs * pairs * 2, length, length), BF),
            jax.ShapeDtypeStruct((tokens, pairs * 2 * HEAD), F32),
        ],
        (seqs, pairs),
        "attend",
        cost(3.5 * seqs * pairs),
        aliases={3: 0},
    )


def attend_back_kernel(
    q_ref, k_ref, v_ref, grad_ref, mixed_ref, inv_ref, probs_ref, out_ref, *, tq
):
    length = q_ref.shape[0]
    lane = lax.broadcasted_iota(jnp.int32, (1, 2 * HEAD), 1)
    keys, values = k_ref[...], v_ref[...]
    scale = HEAD**-0.5
    held = [None] * (length // tq)
    key_parts, value_parts = [], []
    for head in range(2):
        mask = lane // HEAD == head
        grad_k, grad_v = None, None
        cut = slice(head * HEAD, (head + 1) * HEAD)
        for tile in range(length // tq):
            rows = slice(tile * tq, (tile + 1) * tq)
            grad = grad_ref[rows, :]
            inv = inv_ref[rows, :]
            wide = grad.astype(F32)
            inner = jnp.sum(
                jnp.where(mask, wide * mixed_ref[0, rows, :].astype(F32), 0.0), axis=1, keepdims=True
            )
            grad_probs = dot(jnp.where(mask, grad, jnp.zeros_like(grad)), values, NT)
            raised = probs_ref[head, rows, :]
            grad_scores = (raised.astype(F32) * (grad_probs - inner)).astype(BF)
            grad_q = dot(grad_scores, keys) * (inv * scale)
            if head == 0:
                held[tile] = grad_q
            else:
                out_ref[0, rows, :] = jnp.where(lane < HEAD, held[tile], grad_q).astype(BF)
            query = (q_ref[rows, :].astype(F32) * (inv * scale)).T[cut, :].astype(BF)
            outer = (wide * inv).T[cut, :].astype(BF)
            part_k, part_v = dot(query, grad_scores), dot(outer, raised)
            grad_k = part_k if grad_k is None else grad_k + part_k
            grad_v = part_v if grad_v is None else grad_v + part_v
        key_parts.append(grad_k)
        value_parts.append(grad_v)
    out_ref[1] = jnp.concatenate(key_parts, axis=0).T.astype(BF)
    out_ref[2] = jnp.concatenate(value_parts, axis=0).T.astype(BF)


def attend_back(packed, grad_mixed, lefts, inv, probs, length, first, count, held, tq=256):
    pairs = packed.shape[1] // (6 * HEAD)
    at = lambda i: ((first + i) // pairs, (first + i) % pairs)
    spec = lambda part: pl.BlockSpec(
        (length, 2 * HEAD), lambda i: (at(i)[0], part * pairs + at(i)[1])
    )
    return launch(
        ignoring(functools.partial(attend_back_kernel, tq=tq), 7, 1),
        [packed, packed, packed, grad_mixed, lefts, inv, probs, held],
        [
            spec(0), spec(1), spec(2), spec(0),
            pl.BlockSpec((1, length, 2 * HEAD), lambda i: (1, *at(i))), spec(0),
            pl.BlockSpec((2, length, length), lambda i: (first + i, 0, 0)),
        ]
        + anywhere(1),
        [pl.BlockSpec((3, length, 2 * HEAD), lambda i: (0, *at(i)))],
        [jax.ShapeDtypeStruct(held.shape, BF)],
        (count,),
        "attend_back",
        cost(4.5 * count),
        aliases={7: 0},
    )[0]


def forward_kernel(
    scal_ref, mixed_ref, stream_ref, word_ref, wout_ref, gain_ref, wup_ref, wdown_ref, whead_ref,
    mid_ref, mlp_ref, act_ref, slope_ref, out_ref, gpred_ref, branch_ref, ghead_ref,
    *, tiles, step,
):
    index = pl.program_id(0)
    seq = index // tiles
    mid = stream_ref[...] + dot(mixed_ref[0], wout_ref[...])
    mid_ref[...] = mid
    mlp = (normalise(mid)[0] * gain_ref[...]).astype(BF)
    mlp_ref[...] = mlp
    total = mid
    for start in range(0, wup_ref.shape[1], step):
        cols = slice(start, start + step)
        up = dot(mlp, wup_ref[:, cols])
        inner = (2.0 * GELU_A * GELU_B) * (up * up) + 2.0 * GELU_A
        share = 0.5 + 0.5 * jnp.tanh(up * (0.5 * inner))
        full = up * share
        act = full.astype(BF)
        act_ref[:, cols] = act
        slope = share + full * (1.0 - share) * (3.0 * inner - 4.0 * GELU_A)
        slope_ref[:, cols] = slope.astype(BF)
        total = total + dot(act, wdown_ref[cols, :])
    low = total.astype(BF)
    out_ref[...] = low
    scal = scal_ref[pl.ds(seq, 1), :]
    clean = word_ref[...].astype(F32) * scal[:, 3:4]
    gpred = (dot(low, whead_ref[...]) - clean) * scal[:, 2:3]
    gpred_ref[...] = gpred
    gpred_low = gpred.astype(BF)
    branch_ref[...] = dot(gpred_low, whead_ref[...], NT).astype(BF)
    accumulate(ghead_ref, index == 0, dot(gpred.T.astype(BF), low))


def forward(scal, lefts, stream, word, w_out, gain, w_up, w_down, w_head, length, tm=256, step=768):
    tokens, model = stream.shape
    inner, width = w_up.shape[1], w_head.shape[1]
    row = lambda cols: pl.BlockSpec((tm, cols), lambda i: (i, 0))
    shape = lambda cols, kind: jax.ShapeDtypeStruct((tokens, cols), kind)
    return launch(
        functools.partial(forward_kernel, tiles=length // tm, step=step),
        [scal, lefts, stream, word, w_out, gain, w_up, w_down, w_head],
        [
            whole(scal.shape), pl.BlockSpec((1, tm, model), lambda i: (1, i, 0)), row(model), row(width),
            whole(w_out.shape), whole(gain.shape), whole(w_up.shape), whole(w_down.shape),
            whole(w_head.shape),
        ],
        [
            row(model), row(model), row(inner), row(inner), row(model), row(width), row(model),
            pl.BlockSpec((width, model), lambda i: (0, 0)),
        ],
        [
            shape(model, F32), shape(model, BF), shape(inner, BF), shape(inner, BF),
            shape(model, BF), shape(width, F32), shape(model, BF),
            jax.ShapeDtypeStruct((width, model), F32),
        ],
        (tokens // tm,),
        "feed_forward",
        cost(tokens / 45),
    )


def back_kernel(
    mid_ref, slope_ref, gpred_ref, branch_ref, wout_ref, gain_ref, wup_ref, wdown_ref, whead_ref,
    upin_ref, gmid_ref, gattn_ref, gmixed_ref, ggain_ref, *, step,
):
    index = pl.program_id(0)
    branch = branch_ref[...]
    grad = None
    for start in range(0, wup_ref.shape[1], step):
        cols = slice(start, start + step)
        upin = (dot(branch, wdown_ref[cols, :], NT) * slope_ref[:, cols].astype(F32)).astype(BF)
        upin_ref[:, cols] = upin
        part = dot(upin, wup_ref[:, cols], NT)
        grad = part if grad is None else grad + part
    part, gain_part = norm_back(mid_ref[...], gain_ref[...], grad)
    accumulate(ggain_ref, index == 0, gain_part)
    gmid = dot(gpred_ref[...].astype(BF), whead_ref[...], NT) + part
    gmid_ref[...] = gmid
    low = gmid.astype(BF)
    gattn_ref[0] = low
    gmixed_ref[...] = dot(low, wout_ref[...], NT).astype(BF)


def back(mid, slope, gpred, branch, w_out, gain, w_up, w_down, w_head, tm=256, step=768):
    tokens, model = mid.shape
    inner, width = w_up.shape[1], w_head.shape[1]
    row = lambda cols: pl.BlockSpec((tm, cols), lambda i: (i, 0))
    shape = lambda cols, kind: jax.ShapeDtypeStruct((tokens, cols), kind)
    return launch(
        functools.partial(back_kernel, step=step),
        [mid, slope, gpred, branch, w_out, gain, w_up, w_down, w_head],
        [
            row(model), row(inner), row(width), row(model), whole(w_out.shape), whole(gain.shape),
            whole(w_up.shape), whole(w_down.shape), whole(w_head.shape),
        ],
        [
            row(inner), row(model), pl.BlockSpec((1, tm, model), lambda i: (3, i, 0)), row(model),
            pl.BlockSpec((1, model), lambda i: (0, 0)),
        ],
        [
            shape(inner, BF), shape(model, F32), jax.ShapeDtypeStruct((4, tokens, model), BF),
            shape(model, BF), jax.ShapeDtypeStruct((1, model), F32),
        ],
        (tokens // tm,),
        "feed_forward_back",
        cost(tokens / 55),
    )


def input_back_kernel(
    scal_ref, gmid_ref, dq_ref, dk_ref, dv_ref, stream_ref, noisy_ref, word_ref, gpred_ref, gain_ref,
    wqkv_ref, win_ref, gpos_ref, gtime_ref, ggain_ref, gwin_ref, grows_ref, gscale_ref,
):
    tile, seq = pl.program_id(0), pl.program_id(1)
    first = jnp.logical_and(tile == 0, seq == 0)
    model = win_ref.shape[1]
    grad = (
        dot(dq_ref[0], wqkv_ref[:, :model], NT)
        + dot(dk_ref[0], wqkv_ref[:, model : 2 * model], NT)
        + dot(dv_ref[0], wqkv_ref[:, 2 * model :], NT)
    )
    part, gain_part = norm_back(stream_ref[...], gain_ref[...], grad)
    accumulate(ggain_ref, first, gain_part)
    gin = gmid_ref[...] + part
    accumulate(gpos_ref, seq == 0, gin)
    sums = jnp.sum(gin, axis=0, keepdims=True)
    @pl.when(tile == 0)
    def _():
        gtime_ref[pl.ds(seq, 1), :] = sums

    @pl.when(tile > 0)
    def _():
        gtime_ref[pl.ds(seq, 1), :] += sums

    low = gin.astype(BF)
    accumulate(gwin_ref, first, dot(noisy_ref[...].astype(F32).T.astype(BF), low))
    scal = scal_ref[pl.ds(seq, 1), :]
    gclean = scal[:, 0:1] * dot(low, win_ref[...], NT) - gpred_ref[...]
    grows_ref[...] = (gclean * scal[:, 3:4]).astype(BF)
    accumulate(
        gscale_ref, first, jnp.sum(word_ref[...].astype(F32) * gclean, axis=0, keepdims=True)
    )


def input_back(scal, gmid, grads, stream, noisy, word, gpred, gain, w_qkv, w_in, length, tm=256):
    tokens, model = gmid.shape
    width = w_in.shape[0]
    seqs, tiles = tokens // length, length // tm
    row = lambda cols: pl.BlockSpec((tm, cols), lambda i, s: (s * tiles + i, 0))
    plane = lambda part: pl.BlockSpec((1, tm, model), lambda i, s: (part, s * tiles + i, 0))
    fixed = lambda rows, cols: pl.BlockSpec((rows, cols), lambda i, s: (0, 0))
    return launch(
        input_back_kernel,
        [scal, gmid, grads, grads, grads, stream, noisy, word, gpred, gain, w_qkv, w_in],
        [
            whole(scal.shape), row(model), plane(0), plane(1), plane(2), row(model), row(width),
            row(width), row(width), whole(gain.shape), whole(w_qkv.shape), whole(w_in.shape),
        ],
        [
            pl.BlockSpec((tm, model), lambda i, s: (i, 0)), fixed(seqs, model), fixed(1, model),
            fixed(width, model), row(width), fixed(1, width),
        ],
        [
            jax.ShapeDtypeStruct((length, model), F32),
            jax.ShapeDtypeStruct((seqs, model), F32),
            jax.ShapeDtypeStruct((1, model), F32),
            jax.ShapeDtypeStruct((width, model), F32),
            jax.ShapeDtypeStruct((tokens, width), BF),
            jax.ShapeDtypeStruct((1, width), F32),
        ],
        (tiles, seqs),
        "input_back",
        cost(tokens / 90),
    )


def bit_orders(batch):
    bits = list(range(batch.bit_length() - 1))
    return bits, bits[1:3] + bits[:1] + bits[3:]


def place(owner, me, order):
    apart = jnp.bitwise_xor(owner, me)
    spot = 0
    for bit in order:
        spot = spot * 2 + jnp.bitwise_and(lax.shift_right_logical(apart, bit), 1)
    return spot


def chunk_shape(batch, rows, cols):
    row_blocks = min(batch, 16 if batch <= 16 else 32)
    return row_blocks, rows // row_blocks, cols * row_blocks // batch


def outer_kernel(where, left_ref, right_ref, *outs, orders, row_blocks, tw, steps):
    me, core = where[0], where[1]
    acc = dot(left_ref[0], right_ref[0], TN)
    if len(outs) == 1:
        rows = outs[0].shape[2]
        for row in range(row_blocks):
            outs[0][row, 0] = acc[row * rows : (row + 1) * rows, :]
        return
    chunks, rows, cols = outs[0].shape
    col_blocks = chunks // row_blocks
    tile, per = pl.program_id(0), cols // tw
    half, step = tile // steps, tile % steps
    block = step // per if col_blocks > 1 else 0
    cut = pl.ds(pl.multiple_of((step % per) * tw, 128), tw) if col_blocks > 1 else slice(None)

    def write(ref):
        for row in range(row_blocks):
            owner = row * col_blocks + block
            spot = jnp.where(half == 0, place(owner, me, orders[0]), place(owner, me, orders[1]))
            ref[spot, :, cut] = acc[row * rows : (row + 1) * rows, :].astype(ref.dtype)

    @pl.when(core == half)
    def _():
        write(outs[0])

    @pl.when(core != half)
    def _():
        write(outs[1])


def outer(where, lefts, rights, batch, tw=768, by_device=False):
    _, tokens, rows = lefts.shape
    planes, _, width = rights.shape
    cols = planes * width
    row_blocks, chunk_rows, chunk_cols = chunk_shape(batch, rows, cols // 2)
    col_blocks = batch // row_blocks
    tw = next(size for size in (tw, 384, 256, 128) if chunk_cols % size == 0 and width % size == 0)
    per, steps, inside = width // tw, cols // 2 // tw, chunk_cols // tw
    left = lambda i, w: (jnp.where(i // per == planes - 1, lefts.shape[0] - 1, 0), 0, 0)
    if by_device:
        shapes = [jax.ShapeDtypeStruct((row_blocks, col_blocks * 2, chunk_rows, chunk_cols), F32)]
        at = lambda i, w: (0, (i % steps) // inside * 2 + i // steps, 0, i % inside)
        specs = [pl.BlockSpec((row_blocks, 1, chunk_rows, tw), at)]
    else:
        shape = (batch, chunk_rows, chunk_cols)
        shapes = [jax.ShapeDtypeStruct(shape, BF)] * 2
        early = lambda i: jnp.minimum(i, steps - 1)
        late = lambda i: jnp.maximum(i - steps, 0)
        specs = [
            pl.BlockSpec(
                (batch, chunk_rows, tw), lambda i, w: (0, 0, jnp.where(w[1] == 0, early(i), late(i)))
            ),
            pl.BlockSpec(
                (batch, chunk_rows, tw), lambda i, w: (0, 0, jnp.where(w[1] == 0, late(i), early(i)))
            ),
        ]
        if col_blocks > 1:
            specs = [whole(shape)] * 2
    return launch(
        functools.partial(
            outer_kernel, orders=bit_orders(batch), row_blocks=row_blocks, tw=tw, steps=steps
        ),
        [lefts, rights],
        [
            pl.BlockSpec((1, tokens, rows), left),
            pl.BlockSpec((1, tokens, tw), lambda i, w: (i // per, 0, i % per)),
        ],
        specs,
        shapes,
        (cols // tw,),
        "weight_grad",
        cost(tokens / 120),
        prefetch=[where],
    )


def swap(array):
    return lax.ppermute(array, "seq", [(0, 1), (1, 0)])


def hop(array, step):
    batch = lax.axis_size("batch")
    orders = bit_orders(batch)
    pairs = [
        (2 * me + core, 2 * (me ^ (1 << orders[core][step])) + core)
        for me in range(batch)
        for core in range(2)
    ]
    return lax.ppermute(array, ("batch", "seq"), pairs)


def fold_kernel(keep_ref, got_ref, *outs):
    count = keep_ref.shape[0] // 2
    if not count:
        outs[0][...] = (keep_ref[0] + got_ref[0].astype(F32)).astype(outs[0].dtype)
        return
    outs[0][...] = (keep_ref[count:] + got_ref[count:].astype(F32)).astype(BF)
    outs[1][...] = keep_ref[:count] + got_ref[:count].astype(F32)


def fold(keep, got, last=BF, micros=0.4, chained=True):
    count, tail = keep.shape[0] // 2, keep.shape[1:]
    if count:
        shapes = [jax.ShapeDtypeStruct((count, *tail), BF), jax.ShapeDtypeStruct((count, *tail), F32)]
    else:
        shapes = [jax.ShapeDtypeStruct(tail, last)]
    out = launch(
        fold_kernel, [keep, got], [whole(keep.shape), whole(got.shape)],
        [whole(shape.shape) for shape in shapes], shapes, (1,), "fold", cost(micros),
        limit=8 * 2**20 + 12 * keep.size, chained=chained,
    )
    return out if count else out[0]


def rounded_kernel(in_ref, out_ref):
    out_ref[...] = in_ref[...].astype(BF)


def rounded(chunk):
    return launch(
        rounded_kernel, [chunk], [whole(chunk.shape)], [whole(chunk.shape)],
        [jax.ShapeDtypeStruct(chunk.shape, BF)], (1,), "rounded", cost(0.4), limit=8 * 2**20, chained=False,
    )[0]


def join_kernel(held_ref, got_ref, out_ref):
    count = held_ref.shape[0]
    out_ref[:count] = held_ref[...]
    out_ref[count:] = got_ref[...]


def join(held, got):
    shape = (2 * held.shape[0], *held.shape[1:])
    return launch(
        join_kernel, [held, got], [whole(held.shape)] * 2, [whole(shape)],
        [jax.ShapeDtypeStruct(shape, held.dtype)], (1,), "join", cost(0.4),
        limit=8 * 2**20 + 8 * held.size,
    )[0]


class Sum:
    def __init__(self, keep, send):
        self.keep, self.got, self.step = keep, swap(send), -1
        self.steps = lax.axis_size("batch").bit_length() - 1
        self.chunk = None

    def fold(self, last=BF, micros=0.4):
        if self.chunk is not None:
            return
        out = fold(self.keep, self.got, last, micros)
        self.step += 1
        if self.step == self.steps:
            self.chunk = out
        else:
            self.keep = out[1]
            self.got = hop(out[0], self.step)

    def rest(self):
        while self.step < self.steps - 1:
            self.fold()
        return fold(self.keep, self.got, chained=False)

    def finish(self, last=BF):
        while self.chunk is None:
            self.fold(last)
        return self.chunk


class Gather:
    def __init__(self, chunk, batch):
        self.held, self.other = chunk[None], None
        self.steps = list(reversed(range(batch.bit_length() - 1)))
        self.got = hop(self.held, self.steps[0])

    def join(self, plain=False):
        if self.other is not None:
            return
        if plain:
            self.held = jnp.concatenate([self.held, self.got], axis=0)
        else:
            self.held = join(self.held, self.got)
        self.steps.pop(0)
        if self.steps:
            self.got = hop(self.held, self.steps[0])
        else:
            self.other = swap(self.held)

    def finish(self, plain=False):
        while self.other is None:
            self.join(plain)
        return self.held, self.other


def share(chunk):
    return lax.all_gather(chunk, ("batch", "seq"), axis=0)


def mend_kernel(where, own_ref, other_ref, out_ref, *, seqs):
    ours = pl.program_id(0) // seqs == where[1]

    @pl.when(ours)
    def _():
        out_ref[...] = own_ref[...]

    @pl.when(jnp.logical_not(ours))
    def _():
        out_ref[...] = other_ref[...]


def mend(where, own, other):
    seqs, half_len, model = other.shape
    block = (1, half_len, model)
    return launch(
        functools.partial(mend_kernel, seqs=seqs),
        [own, other],
        [
            pl.BlockSpec(block, lambda i, w: (i % seqs, w[1], 0)),
            pl.BlockSpec(block, lambda i, w: (i % seqs, 0, 0)),
        ],
        [pl.BlockSpec(block, lambda i, w: (i, 0, 0))],
        [jax.ShapeDtypeStruct((2 * seqs, half_len, model), BF)],
        (2 * seqs,),
        "mend",
        cost(6),
        prefetch=[where],
    )[0]


def spread_kernel(in_ref, out_ref, *, flip):
    row_blocks, _, _, rows, cols = in_ref.shape
    block = in_ref[...].reshape(row_blocks * rows, cols).astype(F32)
    out_ref[...] = block.T if flip else block


def spread(gathered, batch, rows, cols, flip=False):
    row_blocks, chunk_rows, chunk_cols = chunk_shape(batch, rows, cols // 2)
    view = gathered.reshape(row_blocks, batch // row_blocks, 2, chunk_rows, chunk_cols)
    tw = next(size for size in (512, 384, 256, 128) if chunk_cols % size == 0)
    per, half = chunk_cols // tw, cols // 2 // tw
    return launch(
        functools.partial(spread_kernel, flip=flip),
        [view],
        [
            pl.BlockSpec(
                (row_blocks, 1, 1, chunk_rows, tw),
                lambda i: (0, (i % half) // per, i // half, 0, i % per),
            )
        ],
        [
            pl.BlockSpec((tw, rows), lambda i: (i, 0))
            if flip
            else pl.BlockSpec((rows, tw), lambda i: (0, i))
        ],
        [jax.ShapeDtypeStruct((cols, rows) if flip else (rows, cols), F32)],
        (cols // tw,),
        "spread",
        cost(8),
    )[0]


def spread_near_kernel(
    where, own_ref, other_ref, first_ref, second_ref, *, steps, orders, row_blocks, split
):
    me, core = where[0], where[1]
    chunks, rows, tw = own_ref.shape
    col_blocks = chunks // row_blocks
    step = pl.program_id(0)
    block = (step % steps) * col_blocks // steps if col_blocks > 1 else 0
    tile = jnp.where(step < steps, core, 1 - core) * steps + step % steps

    def write(ref, half, out_ref):
        for row in range(row_blocks):
            owner = row * col_blocks + block
            spot = jnp.where(half == 0, place(owner, me, orders[0]), place(owner, me, orders[1]))
            out_ref[row * rows : (row + 1) * rows, :] = ref[spot].astype(F32)

    for ours in (True, False):
        for out_ref, wanted in ((first_ref, tile < split), (second_ref, tile >= split)):

            @pl.when(jnp.logical_and((step < steps) == ours, wanted))
            def _():
                if ours:
                    write(own_ref, core, out_ref)
                else:
                    write(other_ref, 1 - core, out_ref)


def spread_near(where, own, other, rows, widths):
    batch, chunk_rows, chunk_cols = own.shape
    row_blocks = rows // chunk_rows
    tw = next(size for size in (768, 512, 384, 256, 128) if chunk_cols % size == 0)
    steps, per = sum(widths) // 2 // tw, chunk_cols // tw
    split, rest = widths[0] // tw, widths[1] // tw
    tile = lambda i, w: jnp.where(i < steps, w[1], 1 - w[1]) * steps + i % steps
    second = lambda i, w: jnp.where(
        tile(i, w) >= split, tile(i, w) - split, jnp.where(i < steps, 0, rest - 1)
    )
    return launch(
        functools.partial(
            spread_near_kernel, steps=steps, orders=bit_orders(batch), row_blocks=row_blocks, split=split
        ),
        [own, other],
        [
            pl.BlockSpec(
                (batch, chunk_rows, tw), lambda i, w: (0, 0, jnp.minimum(i, steps - 1) % per)
            ),
            pl.BlockSpec(
                (batch, chunk_rows, tw), lambda i, w: (0, 0, jnp.maximum(i - steps, 0) % per)
            ),
        ],
        [
            pl.BlockSpec((rows, tw), lambda i, w: (0, jnp.minimum(tile(i, w), split - 1))),
            pl.BlockSpec((rows, tw), lambda i, w: (0, second(i, w))),
        ],
        [jax.ShapeDtypeStruct((rows, width), F32) for width in widths],
        (2 * steps,),
        "spread_near",
        cost(8),
        prefetch=[where],
    )


def small_plan(rows, devices):
    each = -(-sum(rows) // devices // 16) * 16
    plan = [[] for _ in range(devices)]
    start = 0
    for source, count in enumerate(rows):
        done = 0
        while done < count:
            chunk, at = divmod(start + done, each)
            size = min(count - done, each - at)
            plan[chunk].append((source, done, at, size))
            done += size
        start += count
    return each, plan


def pack_kernel(
    where, buckets, gpos_ref, gwin_ref, ghead_ref, gtime_ref, ggain_a_ref, ggain_m_ref, gscale_ref,
    ids_ref, grows_ref, keep_ref, send_ref, extra_ref, *, each, plan, orders, buckets_in, span,
):
    me, core = where[0], where[1]
    batch = keep_ref.shape[0]
    panels = gpos_ref.shape[1] // 128
    extra_ref[...] = jnp.zeros_like(extra_ref)
    for seq in range(gtime_ref.shape[0]):
        extra_ref[pl.ds(buckets[seq], 1), :] += gtime_ref[seq : seq + 1, :]
    extra_ref[buckets_in : buckets_in + 1, :] = ggain_a_ref[...]
    extra_ref[buckets_in + 1 : buckets_in + 2, :] = ggain_m_ref[...]
    extra_ref[buckets_in + 2 : buckets_in + 3, :128] = gscale_ref[...]
    sources = (gpos_ref, gwin_ref, ghead_ref, extra_ref)
    for chunk, pieces in enumerate(plan):
        half, owner = divmod(chunk, batch)
        spot = place(owner, me, orders[half])

        def write(ref):
            for panel in range(panels):
                base = panel * each
                filled = 0
                for source, first, at, size in pieces:
                    ref[spot, base + at : base + at + size, :] = sources[source][
                        first : first + size, panel * 128 : (panel + 1) * 128
                    ].astype(ref.dtype)
                    filled = at + size
                if filled < each:
                    ref[spot, base + filled : base + each, :] = jnp.zeros(
                        (each - filled, 128), ref.dtype
                    )

        @pl.when(core == half)
        def _():
            write(keep_ref)

        @pl.when(core != half)
        def _():
            write(send_ref)


    grows = grows_ref[...]
    per = min(4, batch)
    below = slice(panels * each, None)

    def gather_rows(index, _):
        start = index * per * 2 * span
        row = lax.broadcasted_iota(jnp.int32, (per * 2 * span, ids_ref.shape[1]), 0) + start
        one = jnp.where(row == ids_ref[...], 1.0, 0.0).astype(BF)
        sums = dot(one, grows)
        for owner in range(per):
            for half in range(2):
                part = sums[(owner * 2 + half) * span : (owner * 2 + half + 1) * span, :]
                spot = place(index * per + owner, me, orders[half])

                @pl.when(core == half)
                def _():
                    keep_ref[spot, below, :] = part

                @pl.when(core != half)
                def _():
                    send_ref[spot, below, :] = part.astype(BF)

        return 0

    lax.fori_loop(0, batch // per, gather_rows, 0)


def small_rows(length, width, bucket_count):
    return [length, width, width, -(-(bucket_count + 3) // 16) * 16]


def pack(
    where, buckets, gpos, gwin, ghead, gtime, ggain_a, ggain_m, gscale, ids, grows, batch, span,
    bucket_count,
):
    model, width = gpos.shape[1], gwin.shape[0]
    rows = small_rows(gpos.shape[0], width, bucket_count)
    each, plan = small_plan(rows, 2 * batch)
    shape = (batch, each * (model // 128) + span, 128)
    arrays = [gpos, gwin, ghead, gtime, ggain_a, ggain_m, gscale, ids, grows]
    return launch(
        functools.partial(
            pack_kernel, each=each, plan=plan, orders=bit_orders(batch), buckets_in=bucket_count,
            span=span,
        ),
        arrays,
        [whole(array.shape) for array in arrays],
        [whole(shape)] * 2,
        [jax.ShapeDtypeStruct(shape, F32), jax.ShapeDtypeStruct(shape, BF)],
        (1,),
        "pack_small",
        cost(12),
        prefetch=[where, buckets],
        scratch=[pltpu.VMEM((rows[3], model), F32)],
    )


def unpack_kernel(
    where, own_ref, other_ref, mine_ref, table_ref, scal_ref,
    pos_ref, win_ref, head_ref, time_ref, gain_a_ref, gain_m_ref, gtable_ref, turned_ref, extra_ref,
    *, each, plan, orders, vocab,
):
    me, core = where[0], where[1]
    batch = own_ref.shape[0]
    panels = pos_ref.shape[1] // 128
    outs = (pos_ref, win_ref, turned_ref, extra_ref)
    for chunk, pieces in enumerate(plan):
        half, owner = divmod(chunk, batch)
        spot = place(owner, me, orders[half])

        def read(ref):
            for panel in range(panels):
                for source, first, at, size in pieces:
                    base = panel * each + at
                    outs[source][first : first + size, panel * 128 : (panel + 1) * 128] = ref[
                        spot, base : base + size, :
                    ].astype(F32)

        if pieces:

            @pl.when(core == half)
            def _():
                read(own_ref)

            @pl.when(core != half)
            def _():
                read(other_ref)

    head_ref[...] = turned_ref[...].T
    count, width = time_ref.shape[0], table_ref.shape[1]
    time_ref[...] = extra_ref[:count, :]
    gain_a_ref[...] = extra_ref[count, :]
    gain_m_ref[...] = extra_ref[count + 1, :]
    scale = jnp.sum(extra_ref[count + 2 : count + 3, :128], axis=1, keepdims=True)
    mean_norm = scal_ref[0:1, 4:5]
    grad_mean = -math.sqrt(width) / (mean_norm * mean_norm) * scale
    table = table_ref[...].astype(F32)
    norms = jnp.sqrt(jnp.sum(table * table, axis=1, keepdims=True) + 1e-06)
    gtable_ref[...] = mine_ref[: table.shape[0], :] + grad_mean / vocab * table / norms


def unpack(where, own, other, mine, table, scal, length, model, bucket_count, vocab):
    batch = own.shape[0]
    width = table.shape[1]
    rows = small_rows(length, width, bucket_count)
    each, plan = small_plan(rows, 2 * batch)
    shapes = [
        (length, model), (width, model), (model, width), (bucket_count, model), (model,), (model,),
        table.shape,
    ]
    arrays = [own, other, mine, table, scal]
    return launch(
        functools.partial(unpack_kernel, each=each, plan=plan, orders=bit_orders(batch), vocab=vocab),
        arrays,
        [whole(array.shape) for array in arrays],
        [whole(shape) for shape in shapes],
        [jax.ShapeDtypeStruct(shape, F32) for shape in shapes],
        (1,),
        "unpack_small",
        cost(5),
        prefetch=[where],
        scratch=[pltpu.VMEM((width, model), F32), pltpu.VMEM((rows[3], model), F32)],
    )


def local(
    word_ids, buckets, noise, table, w_in, time_table, pos_table, gain_attn, w_qkv, w_out,
    gain_mlp, w_up, w_down, w_head,
):
    ORDER.clear()
    seq_rows, half_len = word_ids.shape
    table_span, embed_width = table.shape
    model = w_qkv.shape[0]
    bucket_count = time_table.shape[0]
    batch, cores = lax.axis_size("batch"), lax.axis_size("seq")
    devices = batch * cores
    vocab = table_span * devices
    length = half_len * cores
    seqs = seq_rows // cores
    tokens = seqs * length
    me = lax.axis_index("batch").astype(jnp.int32)
    core = lax.axis_index("seq").astype(jnp.int32)
    where = jnp.stack([me, core])

    def regroup(array):
        own = lax.dynamic_slice_in_dim(array, core * seqs, seqs, 0)
        other = swap(lax.dynamic_slice_in_dim(array, (1 - core) * seqs, seqs, 0))
        return jnp.concatenate(
            [jnp.where(core == 0, own, other), jnp.where(core == 0, other, own)], axis=1
        )

    bucket_hot = (buckets[:, None] == jnp.arange(bucket_count, dtype=jnp.int32)[None, :]).astype(F32)
    span = -(-(table_span + 1) // 16) * 16
    behind = jnp.pad(
        jnp.sum(bucket_hot, axis=0).astype(BF)[None, :],
        ((0, span - table_span - 1), (0, embed_width - bucket_count)),
    )
    own_table, other_table = Gather(jnp.concatenate([table, behind], axis=0), batch).finish(True)
    word_list = regroup(word_ids)
    device = lax.div(word_list, table_span)
    row_in = word_list - device * table_span
    owner, its_core = lax.div(device, cores), lax.rem(device, cores)
    orders = bit_orders(batch)
    spot = jnp.where(its_core == 0, place(owner, me, orders[0]), place(owner, me, orders[1]))
    spot = jnp.where(its_core == core, spot, spot + batch)
    ids = (spot * span + row_in).reshape(1, tokens)
    home = (device * span + row_in).reshape(1, tokens)
    noise_rows = regroup(noise).reshape(tokens, embed_width)
    own_buckets = lax.dynamic_slice_in_dim(buckets, core * seqs, seqs, 0)

    gain_a, gain_m = gain_attn.reshape(1, model), gain_mlp.reshape(1, model)
    word, noisy, stream, lefts, packed, scal = embed(
        own_buckets, ids, own_table, other_table, noise_rows, w_in, time_table, pos_table, gain_a,
        w_qkv, table_span,
    )
    lefts, probs, inv = attend(packed, length, lefts)
    mid, mlp, act, slope, low, gpred, branch, ghead = forward(
        scal, lefts, stream, word, w_out, gain_m, w_up, w_down, w_head, length
    )
    pairs = tokens // length * (packed.shape[1] // (6 * HEAD))
    inner = w_up.shape[1]

    def attend_part(first, last, grads):
        return attend_back(packed, gmixed, lefts, inv, probs, length, first, last - first, grads)

    (down,) = outer(where, branch[None], act[None], batch, 512, by_device=True)
    down_sum = lax.psum_scatter(
        down.reshape(devices, *down.shape[2:]), ("batch", "seq"), scatter_dimension=0, tiled=False
    )
    upin, gmid, grads, gmixed, ggain_m = back(
        mid, slope, gpred, branch, w_out, gain_m, w_up, w_down, w_head
    )
    up = Sum(*outer(where, mlp[None], upin[None], batch, 512))
    grads = attend_part(0, pairs // 2, grads)
    up.fold()
    grads = attend_part(pairs // 2, pairs, grads)
    up.fold()
    attn = Sum(*outer(where, lefts, grads, batch))
    down_all = share(rounded(down_sum))
    up.fold()
    gpos, gtime, ggain_a, gwin, grows, gscale = input_back(
        scal, gmid, grads, stream, noisy, word, gpred, gain_a, w_qkv, w_in, length
    )
    up.fold()
    attn.fold()
    small = Sum(
        *pack(
            where, own_buckets, gpos, gwin, ghead, gtime, ggain_a, ggain_m, gscale, home, grows, batch,
            span, bucket_count,
        )
    )
    up_all = share(up.rest())
    attn.fold(micros=25)
    small.fold(F32)
    low = low.reshape(seqs, length, model)
    output = mend(
        where, low, swap(lax.dynamic_slice_in_dim(low, (1 - core) * half_len, half_len, 1))
    )
    grad_down = spread(down_all, batch, model, inner, True)
    attn.fold()
    small.fold(F32)
    attn.fold()
    small.fold(F32)
    attn_all = Gather(attn.finish(), batch)
    small.fold(F32)
    mine = small.finish(F32)
    cut = mine.shape[0] - span
    small_all = Gather(mine[:cut].astype(BF), batch)
    attn_all.join()
    small_all.join()
    attn_all.join()
    small_all.join()
    attn_all.join()
    small_all.join()
    grad_up = spread(up_all, batch, model, inner)
    small_all.join()
    attn_own, attn_other = attn_all.finish()
    small_own, small_other = small_all.finish()
    grad_qkv, grad_out = spread_near(where, attn_own, attn_other, model, (3 * model, model))
    pos_sum, win_sum, head_sum, time_sum, gain_a_sum, gain_m_sum, grad_table = unpack(
        where, small_own, small_other, mine[cut:], table, scal, length, model, bucket_count, vocab
    )
    return (
        output,
        grad_table,
        win_sum,
        time_sum,
        pos_sum,
        gain_a_sum,
        grad_qkv,
        grad_out,
        gain_m_sum,
        grad_up,
        grad_down,
        head_sum,
        scal[0, 4],
    )


def solution(mesh):
    rows = P(("batch", "seq"), None)
    in_specs = (P("batch", "seq"), P("batch"), P("batch", "seq", None), rows) + (P(),) * 10
    out_specs = (P("batch", "seq", None), rows) + (P(),) * 11
    return jax.shard_map(local, mesh=mesh, in_specs=in_specs, out_specs=out_specs, check_vma=False)
```

```python
import functools
import math

import jax
import jax.numpy as jnp
from jax import lax
from jax.experimental import pallas as pl
from jax.experimental.pallas import tpu as pltpu
from jax.sharding import PartitionSpec as P

HEAD = 64
BF = jnp.bfloat16
F32 = jnp.float32
NN = (((1,), (0,)), ((), ()))
NT = (((1,), (1,)), ((), ()))
TN = (((0,), (0,)), ((), ()))
VMEM_BYTES = 50 * 2**20
GELU_A = math.sqrt(2 / math.pi)
GELU_B = 0.044715


def dot(left, right, dims=NN):
    return lax.dot_general(left, right, dims, preferred_element_type=F32)


def params(limit=VMEM_BYTES):
    return pltpu.CompilerParams(vmem_limit_bytes=limit)


def cost(micros):
    return pl.CostEstimate(flops=int(micros * 1.2e9), bytes_accessed=0, transcendentals=0)


def whole(shape):
    return pl.BlockSpec(shape, lambda *_: (0,) * len(shape), pipeline_mode=pl.Buffered(1))


def smem():
    return pl.BlockSpec(memory_space=pltpu.SMEM)


def normalise(hidden):
    centre = hidden - jnp.mean(hidden, axis=-1, keepdims=True)
    inv = lax.rsqrt(jnp.mean(centre * centre, axis=-1, keepdims=True) + 1e-05)
    return centre * inv, inv


def norm_back(hidden, gain, grad):
    unit, inv = normalise(hidden)
    scaled = grad * gain
    part = inv * (
        scaled
        - jnp.mean(scaled, axis=-1, keepdims=True)
        - unit * jnp.mean(scaled * unit, axis=-1, keepdims=True)
    )
    return part, jnp.sum(grad * unit, axis=0, keepdims=True)


ORDER = []


def launch(kernel, inputs, in_specs, out_specs, out_shape, grid, name, estimate, prefetch=(), aliases=None, scratch=(), limit=VMEM_BYTES, chained=True):
    count = len(prefetch) + len(inputs)
    outs, waits = len(out_shape), len(ORDER)

    def body(*refs):
        at = count + waits
        refs[at + outs][...] = jnp.zeros((8, 128), F32)
        kernel(*refs[:count], *refs[at : at + outs], *refs[at + outs + 1 :])

    token = pl.BlockSpec((8, 128), lambda *_: (0, 0)) if grid else resident(1)[0]
    *results, last = pl.pallas_call(
        body,
        grid_spec=pltpu.PrefetchScalarGridSpec(
            num_scalar_prefetch=len(prefetch),
            grid=grid,
            in_specs=list(in_specs) + anywhere(waits),
            out_specs=list(out_specs) + [token],
            scratch_shapes=list(scratch),
        ),
        out_shape=list(out_shape) + [jax.ShapeDtypeStruct((8, 128), F32)],
        input_output_aliases={len(prefetch) + k: v for k, v in (aliases or {}).items()},
        compiler_params=params(limit),
        cost_estimate=estimate,
        name=name,
    )(*prefetch, *inputs, *ORDER)
    if chained:
        ORDER[:] = [last]
    return results


def resident(count):
    return [pl.BlockSpec(memory_space=pltpu.VMEM)] * count


def anywhere(count):
    return [pl.BlockSpec(memory_space=pl.ANY)] * count


def ignoring(kernel, inputs, extra):
    return lambda *refs: kernel(*refs[:inputs], *refs[inputs + extra :])


def accumulate(ref, first, value):
    @pl.when(first)
    def _():
        ref[...] = value

    @pl.when(jnp.logical_not(first))
    def _():
        ref[...] += value


def embed_kernel(
    where, buckets, ids_ref, own_ref, other_ref, noise_ref, win_ref, time_ref, pos_ref, gain_ref, wqkv_ref,
    word_ref, noisy_ref, stream_ref, left_ref, packed_ref, scal_ref, table_ref,
    *, tiles, table_span, seqs, step,
):
    index = pl.program_id(0)
    seq = index // tiles
    first = where[1] * seqs
    chunks, span, width = own_ref.shape
    bucket_count = time_ref.shape[0]

    @pl.when(index == 0)
    def _():
        real = lax.broadcasted_iota(jnp.int32, (span, 1), 0) < table_span
        norms = jnp.zeros((span, 1), F32)
        counts = jnp.zeros((1, width), F32)
        for half, ref in enumerate((own_ref, other_ref)):
            for chunk in range(chunks):
                block = ref[chunk].astype(F32)
                norms += jnp.where(
                    real, jnp.sqrt(jnp.sum(block * block, axis=1, keepdims=True) + 1e-06), 0.0
                )
                counts += block[table_span : table_span + 1, :]
                at = (half * chunks + chunk) * span
                table_ref[:, at : at + span] = block.T.astype(BF)
        mean_norm = jnp.sum(norms, axis=0, keepdims=True) / (2 * chunks * table_span)
        lane = lax.broadcasted_iota(jnp.int32, (1, width), 1)
        scal_ref[...] = jnp.zeros_like(scal_ref)
        for each in range(seqs):
            bucket = buckets[first + each]
            signal, spread = jnp.float32(0.0), jnp.float32(0.0)
            for kind in range(bucket_count):
                angle = math.pi / 2 * (kind + 1.0) / (bucket_count + 1)
                signal = jnp.where(bucket == kind, math.cos(angle), signal)
                spread = jnp.where(bucket == kind, math.sin(angle), spread)
            count = jnp.sum(jnp.where(lane == bucket, counts, 0.0), axis=1, keepdims=True)
            row = jnp.where(lane == 0, signal, jnp.where(lane == 1, spread, 0.0))
            row = jnp.where(lane == 2, 2.0 / count, row)
            row = jnp.where(lane == 3, math.sqrt(width) / mean_norm, row)
            scal_ref[each : each + 1, :] = jnp.where(lane == 4, mean_norm, row)

    ids = ids_ref[...]
    word = jnp.zeros((width, ids.shape[1]), F32)
    for start in range(0, 2 * chunks * span, step):
        row = lax.broadcasted_iota(jnp.int32, (step, ids.shape[1]), 0) + start
        one = jnp.where(row == ids, 1.0, 0.0).astype(BF)
        word += dot(table_ref[:, start : start + step], one)
    word = word.T
    word_ref[...] = word.astype(BF)
    scal = scal_ref[pl.ds(seq, 1), :]
    clean = word * scal[:, 3:4]
    noisy = (scal[:, 0:1] * clean + scal[:, 1:2] * noise_ref[...].astype(F32)).astype(BF)
    noisy_ref[...] = noisy
    stream = dot(noisy, win_ref[...]) + time_ref[pl.ds(buckets[first + seq], 1), :] + pos_ref[...]
    stream_ref[...] = stream
    attn = (normalise(stream)[0] * gain_ref[...].reshape(1, -1)).astype(BF)
    left_ref[0] = attn
    packed_ref[...] = dot(attn, wqkv_ref[...]).astype(BF)


def embed(buckets, ids, own, other, noise, w_in, time_table, pos_table, gain, w_qkv, table_span, where, tm=256):
    tokens, width = noise.shape
    length, model = pos_table.shape
    seqs, tiles = tokens // length, length // tm
    wide = w_qkv.shape[1]
    rows = 2 * own.shape[0] * own.shape[1]
    row = lambda cols: pl.BlockSpec((tm, cols), lambda i, *_: (i, 0))
    return launch(
        functools.partial(
            embed_kernel, tiles=tiles, table_span=table_span, seqs=seqs, step=min(rows, 1024)
        ),
        [ids, own, other, noise, w_in, time_table, pos_table, gain, w_qkv],
        [
            pl.BlockSpec((1, tm), lambda i, *_: (0, i)), whole(own.shape), whole(other.shape),
            row(width), whole(w_in.shape), whole(time_table.shape),
            pl.BlockSpec((tm, model), lambda i, *_: (i % tiles, 0)), whole(gain.shape),
            whole(w_qkv.shape),
        ],
        [
            row(width), row(width), row(model), pl.BlockSpec((1, tm, model), lambda i, *_: (0, i, 0)),
            row(wide), pl.BlockSpec((8, width), lambda *_: (0, 0)),
        ],
        [
            jax.ShapeDtypeStruct((tokens, width), BF),
            jax.ShapeDtypeStruct((tokens, width), BF),
            jax.ShapeDtypeStruct((tokens, model), F32),
            jax.ShapeDtypeStruct((2, tokens, model), BF),
            jax.ShapeDtypeStruct((tokens, wide), BF),
            jax.ShapeDtypeStruct((8, width), F32),
        ],
        (tokens // tm,),
        "embed",
        cost(tokens / 80),
        prefetch=[where, buckets],
        scratch=[pltpu.VMEM((width, rows), BF)],
    )


def attend_kernel(q_ref, k_ref, v_ref, mixed_ref, probs_ref, inv_ref, *, tq):
    length = q_ref.shape[0]
    lane = lax.broadcasted_iota(jnp.int32, (1, 2 * HEAD), 1)
    keys = k_ref[...]
    values = jnp.concatenate([v_ref[...], jnp.ones_like(v_ref[...])], axis=1)
    scale = math.log2(math.e) * HEAD**-0.5
    for start in range(0, length, tq):
        rows = slice(start, start + tq)
        query = q_ref[rows, :]
        parts = []
        for head in range(2):
            own = jnp.where(lane // HEAD == head, query, jnp.zeros_like(query))
            scores = dot(own, keys, NT)
            peak = jnp.max(scores, axis=1, keepdims=True)
            raised = jnp.exp2(scores * scale - peak * scale).astype(BF)
            probs_ref[head, rows, :] = raised
            sums = dot(raised, values)
            inv = 1.0 / sums[:, 2 * HEAD :]
            parts.append((sums[:, : 2 * HEAD] * inv, inv))
        low = lane < HEAD
        mixed_ref[0, rows, :] = jnp.where(low, parts[0][0], parts[1][0]).astype(BF)
        inv_ref[rows, :] = jnp.where(low, parts[0][1], parts[1][1])


def attend(packed, length, lefts, tq=256):
    tokens = packed.shape[0]
    seqs, pairs = tokens // length, packed.shape[1] // (6 * HEAD)
    spec = lambda part: pl.BlockSpec((length, 2 * HEAD), lambda s, j: (s, part * pairs + j))
    return launch(
        ignoring(functools.partial(attend_kernel, tq=tq), 3, 1),
        [packed, packed, packed, lefts],
        [spec(0), spec(1), spec(2)] + anywhere(1),
        [
            pl.BlockSpec((1, length, 2 * HEAD), lambda s, j: (1, s, j)),
            pl.BlockSpec((2, length, length), lambda s, j: (s * pairs + j, 0, 0)), spec(0),
        ],
        [
            jax.ShapeDtypeStruct(lefts.shape, BF),
            jax.ShapeDtypeStruct((seqs * pairs * 2, length, length), BF),
            jax.ShapeDtypeStruct((tokens, pairs * 2 * HEAD), F32),
        ],
        (seqs, pairs),
        "attend",
        cost(3.5 * seqs * pairs),
        aliases={3: 0},
    )


def attend_back_kernel(
    q_ref, k_ref, v_ref, grad_ref, mixed_ref, inv_ref, probs_ref, out_ref, *, tq
):
    length = q_ref.shape[0]
    lane = lax.broadcasted_iota(jnp.int32, (1, 2 * HEAD), 1)
    keys, values = k_ref[...], v_ref[...]
    scale = HEAD**-0.5
    held = [None] * (length // tq)
    key_parts, value_parts = [], []
    for head in range(2):
        mask = lane // HEAD == head
        grad_k, grad_v = None, None
        cut = slice(head * HEAD, (head + 1) * HEAD)
        for tile in range(length // tq):
            rows = slice(tile * tq, (tile + 1) * tq)
            grad = grad_ref[rows, :]
            inv = inv_ref[rows, :]
            wide = grad.astype(F32)
            inner = jnp.sum(
                jnp.where(mask, wide * mixed_ref[0, rows, :].astype(F32), 0.0), axis=1, keepdims=True
            )
            grad_probs = dot(jnp.where(mask, grad, jnp.zeros_like(grad)), values, NT)
            raised = probs_ref[head, rows, :]
            grad_scores = (raised.astype(F32) * (grad_probs - inner)).astype(BF)
            grad_q = dot(grad_scores, keys) * (inv * scale)
            if head == 0:
                held[tile] = grad_q
            else:
                out_ref[0, rows, :] = jnp.where(lane < HEAD, held[tile], grad_q).astype(BF)
            query = (q_ref[rows, :].astype(F32) * (inv * scale)).T[cut, :].astype(BF)
            outer = (wide * inv).T[cut, :].astype(BF)
            part_k, part_v = dot(query, grad_scores), dot(outer, raised)
            grad_k = part_k if grad_k is None else grad_k + part_k
            grad_v = part_v if grad_v is None else grad_v + part_v
        key_parts.append(grad_k)
        value_parts.append(grad_v)
    out_ref[1] = jnp.concatenate(key_parts, axis=0).T.astype(BF)
    out_ref[2] = jnp.concatenate(value_parts, axis=0).T.astype(BF)


def attend_back(packed, grad_mixed, lefts, inv, probs, length, first, count, held, tq=256):
    pairs = packed.shape[1] // (6 * HEAD)
    at = lambda i: ((first + i) // pairs, (first + i) % pairs)
    spec = lambda part: pl.BlockSpec(
        (length, 2 * HEAD), lambda i: (at(i)[0], part * pairs + at(i)[1])
    )
    return launch(
        ignoring(functools.partial(attend_back_kernel, tq=tq), 7, 1),
        [packed, packed, packed, grad_mixed, lefts, inv, probs, held],
        [
            spec(0), spec(1), spec(2), spec(0),
            pl.BlockSpec((1, length, 2 * HEAD), lambda i: (1, *at(i))), spec(0),
            pl.BlockSpec((2, length, length), lambda i: (first + i, 0, 0)),
        ]
        + anywhere(1),
        [pl.BlockSpec((3, length, 2 * HEAD), lambda i: (0, *at(i)))],
        [jax.ShapeDtypeStruct(held.shape, BF)],
        (count,),
        "attend_back",
        cost(4.5 * count), limit=34 * 2**20,
        aliases={7: 0},
    )[0]


def forward_kernel(
    where, scal_ref, mixed_ref, stream_ref, word_ref, wout_ref, gain_ref, wup_ref, wdown_ref, whead_ref,
    mid_ref, mlp_ref, act_ref, slope_ref, ours_ref, theirs_ref, gpred_ref, branch_ref, ghead_ref,
    *, tiles, step,
):
    index = pl.program_id(0)
    seq = index // tiles
    mid = stream_ref[...] + dot(mixed_ref[0], wout_ref[...])
    mid_ref[...] = mid
    mlp = (normalise(mid)[0] * gain_ref[...].reshape(1, -1)).astype(BF)
    mlp_ref[...] = mlp
    total = mid
    for start in range(0, wup_ref.shape[1], step):
        cols = slice(start, start + step)
        up = dot(mlp, wup_ref[:, cols])
        inner = (2.0 * GELU_A * GELU_B) * (up * up) + 2.0 * GELU_A
        share = 0.5 + 0.5 * jnp.tanh(up * (0.5 * inner))
        full = up * share
        act = full.astype(BF)
        act_ref[:, cols] = act
        slope = share + full * (1.0 - share) * (3.0 * inner - 4.0 * GELU_A)
        slope_ref[:, cols] = slope.astype(BF)
        total = total + dot(act, wdown_ref[cols, :])
    low = total.astype(BF)
    half = (index % tiles) // (tiles // 2)

    @pl.when(half == where[1])
    def _():
        ours_ref[0] = low

    @pl.when(half != where[1])
    def _():
        theirs_ref[0] = low

    scal = scal_ref[pl.ds(seq, 1), :]
    clean = word_ref[...].astype(F32) * scal[:, 3:4]
    gpred = (dot(low, whead_ref[...]) - clean) * scal[:, 2:3]
    gpred_ref[...] = gpred
    gpred_low = gpred.astype(BF)
    branch_ref[...] = dot(gpred_low, whead_ref[...], NT).astype(BF)
    accumulate(ghead_ref, index == 0, dot(gpred.T.astype(BF), low))


def forward(where, scal, lefts, stream, word, w_out, gain, w_up, w_down, w_head, length, tm=256, step=768):
    tokens, model = stream.shape
    inner, width = w_up.shape[1], w_head.shape[1]
    row = lambda cols: pl.BlockSpec((tm, cols), lambda i, *_: (i, 0))
    shape = lambda cols, kind: jax.ShapeDtypeStruct((tokens, cols), kind)
    tiles = length // tm
    turn = lambda i, core: (i // tiles, jnp.clip(i % tiles - core * (tiles // 2), 0, tiles // 2 - 1), 0)
    halves = jax.ShapeDtypeStruct((tokens // length, length // 2, model), BF)
    return launch(
        functools.partial(forward_kernel, tiles=tiles, step=step),
        [scal, lefts, stream, word, w_out, gain, w_up, w_down, w_head],
        [
            whole(scal.shape), pl.BlockSpec((1, tm, model), lambda i, *_: (1, i, 0)), row(model), row(width),
            whole(w_out.shape), whole(gain.shape), whole(w_up.shape), whole(w_down.shape),
            whole(w_head.shape),
        ],
        [
            row(model), row(model), row(inner), row(inner),
            pl.BlockSpec((1, tm, model), lambda i, w: turn(i, w[1])),
            pl.BlockSpec((1, tm, model), lambda i, w: turn(i, 1 - w[1])), row(width), row(model),
            pl.BlockSpec((width, model), lambda *_: (0, 0)),
        ],
        [
            shape(model, F32), shape(model, BF), shape(inner, BF), shape(inner, BF),
            halves, halves, shape(width, F32), shape(model, BF),
            jax.ShapeDtypeStruct((width, model), F32),
        ],
        (tokens // tm,),
        "feed_forward",
        cost(tokens / 45),
        prefetch=[where],
    )


def back_kernel(
    mid_ref, slope_ref, gpred_ref, branch_ref, wout_ref, gain_ref, wup_ref, wdown_ref, whead_ref,
    upin_ref, gmid_ref, gattn_ref, gmixed_ref, ggain_ref, *, step,
):
    index = pl.program_id(0)
    branch = branch_ref[...]
    grad = None
    for start in range(0, wup_ref.shape[1], step):
        cols = slice(start, start + step)
        upin = (dot(branch, wdown_ref[cols, :], NT) * slope_ref[:, cols].astype(F32)).astype(BF)
        upin_ref[:, cols] = upin
        part = dot(upin, wup_ref[:, cols], NT)
        grad = part if grad is None else grad + part
    part, gain_part = norm_back(mid_ref[...], gain_ref[...].reshape(1, -1), grad)
    accumulate(ggain_ref, index == 0, gain_part)
    gmid = dot(gpred_ref[...].astype(BF), whead_ref[...], NT) + part
    gmid_ref[...] = gmid
    low = gmid.astype(BF)
    gattn_ref[0] = low
    gmixed_ref[...] = dot(low, wout_ref[...], NT).astype(BF)


def back(mid, slope, gpred, branch, w_out, gain, w_up, w_down, w_head, tm=256, step=768):
    tokens, model = mid.shape
    inner, width = w_up.shape[1], w_head.shape[1]
    row = lambda cols: pl.BlockSpec((tm, cols), lambda i: (i, 0))
    shape = lambda cols, kind: jax.ShapeDtypeStruct((tokens, cols), kind)
    return launch(
        functools.partial(back_kernel, step=step),
        [mid, slope, gpred, branch, w_out, gain, w_up, w_down, w_head],
        [
            row(model), row(inner), row(width), row(model), whole(w_out.shape), whole(gain.shape),
            whole(w_up.shape), whole(w_down.shape), whole(w_head.shape),
        ],
        [
            row(inner), row(model), pl.BlockSpec((1, tm, model), lambda i: (3, i, 0)), row(model),
            pl.BlockSpec((1, model), lambda i: (0, 0)),
        ],
        [
            shape(inner, BF), shape(model, F32), jax.ShapeDtypeStruct((4, tokens, model), BF),
            shape(model, BF), jax.ShapeDtypeStruct((1, model), F32),
        ],
        (tokens // tm,),
        "feed_forward_back",
        cost(tokens / 55),
    )


def input_back_kernel(
    scal_ref, gmid_ref, dq_ref, dk_ref, dv_ref, stream_ref, noisy_ref, word_ref, gpred_ref, gain_ref,
    wqkv_ref, win_ref, gpos_ref, gtime_ref, ggain_ref, gwin_ref, grows_ref, gscale_ref,
):
    tile, seq = pl.program_id(0), pl.program_id(1)
    first = jnp.logical_and(tile == 0, seq == 0)
    model = win_ref.shape[1]
    grad = (
        dot(dq_ref[0], wqkv_ref[:, :model], NT)
        + dot(dk_ref[0], wqkv_ref[:, model : 2 * model], NT)
        + dot(dv_ref[0], wqkv_ref[:, 2 * model :], NT)
    )
    part, gain_part = norm_back(stream_ref[...], gain_ref[...].reshape(1, -1), grad)
    accumulate(ggain_ref, first, gain_part)
    gin = gmid_ref[...] + part
    accumulate(gpos_ref, seq == 0, gin)
    sums = jnp.sum(gin, axis=0, keepdims=True)
    @pl.when(tile == 0)
    def _():
        gtime_ref[pl.ds(seq, 1), :] = sums

    @pl.when(tile > 0)
    def _():
        gtime_ref[pl.ds(seq, 1), :] += sums

    low = gin.astype(BF)
    accumulate(gwin_ref, first, dot(noisy_ref[...].astype(F32).T.astype(BF), low))
    scal = scal_ref[pl.ds(seq, 1), :]
    gclean = scal[:, 0:1] * dot(low, win_ref[...], NT) - gpred_ref[...]
    grows_ref[...] = (gclean * scal[:, 3:4]).astype(BF)
    accumulate(
        gscale_ref, first, jnp.sum(word_ref[...].astype(F32) * gclean, axis=0, keepdims=True)
    )


def input_back(scal, gmid, grads, stream, noisy, word, gpred, gain, w_qkv, w_in, length, tm=256):
    tokens, model = gmid.shape
    width = w_in.shape[0]
    seqs, tiles = tokens // length, length // tm
    row = lambda cols: pl.BlockSpec((tm, cols), lambda i, s: (s * tiles + i, 0))
    plane = lambda part: pl.BlockSpec((1, tm, model), lambda i, s: (part, s * tiles + i, 0))
    fixed = lambda rows, cols: pl.BlockSpec((rows, cols), lambda i, s: (0, 0))
    return launch(
        input_back_kernel,
        [scal, gmid, grads, grads, grads, stream, noisy, word, gpred, gain, w_qkv, w_in],
        [
            whole(scal.shape), row(model), plane(0), plane(1), plane(2), row(model), row(width),
            row(width), row(width), whole(gain.shape), whole(w_qkv.shape), whole(w_in.shape),
        ],
        [
            pl.BlockSpec((tm, model), lambda i, s: (i, 0)), fixed(seqs, model), fixed(1, model),
            fixed(width, model), row(width), fixed(1, width),
        ],
        [
            jax.ShapeDtypeStruct((length, model), F32),
            jax.ShapeDtypeStruct((seqs, model), F32),
            jax.ShapeDtypeStruct((1, model), F32),
            jax.ShapeDtypeStruct((width, model), F32),
            jax.ShapeDtypeStruct((tokens, width), BF),
            jax.ShapeDtypeStruct((1, width), F32),
        ],
        (tiles, seqs),
        "input_back",
        cost(tokens / 90), limit=34 * 2**20,
    )


def bit_orders(batch):
    bits = list(range(batch.bit_length() - 1))
    return bits, bits[1:3] + bits[:1] + bits[3:]


def place(owner, me, order):
    apart = jnp.bitwise_xor(owner, me)
    spot = 0
    for bit in order:
        spot = spot * 2 + jnp.bitwise_and(lax.shift_right_logical(apart, bit), 1)
    return spot


def chunk_shape(batch, rows, cols):
    row_blocks = min(batch, 16 if batch <= 16 else 32)
    return row_blocks, rows // row_blocks, cols * row_blocks // batch


def outer_kernel(where, left_ref, right_ref, *outs, orders, row_blocks, tw, steps):
    me, core = where[0], where[1]
    acc = dot(left_ref[0], right_ref[0], TN)
    if len(outs) == 1:
        rows = outs[0].shape[2]
        for row in range(row_blocks):
            outs[0][row, 0] = acc[row * rows : (row + 1) * rows, :]
        return
    chunks, rows, cols = outs[0].shape
    col_blocks = chunks // row_blocks
    tile, per = pl.program_id(0), cols // tw
    half, step = tile // steps, tile % steps
    block = step // per if col_blocks > 1 else 0
    cut = pl.ds(pl.multiple_of((step % per) * tw, 128), tw) if col_blocks > 1 else slice(None)

    def write(ref):
        for row in range(row_blocks):
            owner = row * col_blocks + block
            spot = jnp.where(half == 0, place(owner, me, orders[0]), place(owner, me, orders[1]))
            ref[spot, :, cut] = acc[row * rows : (row + 1) * rows, :].astype(ref.dtype)

    @pl.when(core == half)
    def _():
        write(outs[0])

    @pl.when(core != half)
    def _():
        write(outs[1])


def outer(where, lefts, rights, batch, tw=768, by_device=False):
    _, tokens, rows = lefts.shape
    planes, _, width = rights.shape
    cols = planes * width
    row_blocks, chunk_rows, chunk_cols = chunk_shape(batch, rows, cols // 2)
    col_blocks = batch // row_blocks
    tw = next(size for size in (tw, 384, 256, 128) if chunk_cols % size == 0 and width % size == 0)
    per, steps, inside = width // tw, cols // 2 // tw, chunk_cols // tw
    left = lambda i, w: (jnp.where(i // per == planes - 1, lefts.shape[0] - 1, 0), 0, 0)
    if by_device:
        shapes = [jax.ShapeDtypeStruct((row_blocks, col_blocks * 2, chunk_rows, chunk_cols), F32)]
        at = lambda i, w: (0, (i % steps) // inside * 2 + i // steps, 0, i % inside)
        specs = [pl.BlockSpec((row_blocks, 1, chunk_rows, tw), at)]
    else:
        shape = (batch, chunk_rows, chunk_cols)
        shapes = [jax.ShapeDtypeStruct(shape, BF)] * 2
        early = lambda i: jnp.minimum(i, steps - 1)
        late = lambda i: jnp.maximum(i - steps, 0)
        specs = [
            pl.BlockSpec(
                (batch, chunk_rows, tw), lambda i, w: (0, 0, jnp.where(w[1] == 0, early(i), late(i)))
            ),
            pl.BlockSpec(
                (batch, chunk_rows, tw), lambda i, w: (0, 0, jnp.where(w[1] == 0, late(i), early(i)))
            ),
        ]
        if col_blocks > 1:
            specs = [whole(shape)] * 2
    return launch(
        functools.partial(
            outer_kernel, orders=bit_orders(batch), row_blocks=row_blocks, tw=tw, steps=steps
        ),
        [lefts, rights],
        [
            pl.BlockSpec((1, tokens, rows), left),
            pl.BlockSpec((1, tokens, tw), lambda i, w: (i // per, 0, i % per)),
        ],
        specs,
        shapes,
        (cols // tw,),
        "weight_grad",
        cost(tokens / 120),
        prefetch=[where],
    )


def swap(array):
    return lax.ppermute(array, "seq", [(0, 1), (1, 0)])


def hop(array, step):
    batch = lax.axis_size("batch")
    orders = bit_orders(batch)
    pairs = [
        (2 * me + core, 2 * (me ^ (1 << orders[core][step])) + core)
        for me in range(batch)
        for core in range(2)
    ]
    return lax.ppermute(array, ("batch", "seq"), pairs)


def fold_kernel(keep_ref, got_ref, *outs):
    count = keep_ref.shape[0] // 2
    if not count:
        outs[0][...] = (keep_ref[0] + got_ref[0].astype(F32)).astype(outs[0].dtype)
        return
    outs[0][...] = (keep_ref[count:] + got_ref[count:].astype(F32)).astype(BF)
    outs[1][...] = keep_ref[:count] + got_ref[:count].astype(F32)


def fold(keep, got, last=BF, micros=0.4, chained=True):
    count, tail = keep.shape[0] // 2, keep.shape[1:]
    if count:
        shapes = [jax.ShapeDtypeStruct((count, *tail), BF), jax.ShapeDtypeStruct((count, *tail), F32)]
    else:
        shapes = [jax.ShapeDtypeStruct(tail, last)]
    out = launch(
        fold_kernel, [keep, got], resident(2), resident(len(shapes)), shapes, (), "fold", cost(micros),
        limit=8 * 2**20 + 12 * keep.size, chained=chained,
    )
    return out if count else out[0]


def rounded_kernel(in_ref, out_ref):
    out_ref[...] = in_ref[...].astype(BF)


def rounded(chunk):
    return launch(
        rounded_kernel, [chunk], [whole(chunk.shape)], [whole(chunk.shape)],
        [jax.ShapeDtypeStruct(chunk.shape, BF)], (1,), "rounded", cost(0.4), limit=8 * 2**20, chained=False,
    )[0]


def join_kernel(held_ref, got_ref, out_ref):
    count = held_ref.shape[0]
    out_ref[:count] = held_ref[...]
    out_ref[count:] = got_ref[...]


def join(held, got, micros):
    shape = (2 * held.shape[0], *held.shape[1:])
    return launch(
        join_kernel, [held, got], resident(2), resident(1),
        [jax.ShapeDtypeStruct(shape, held.dtype)], (), "join", cost(micros),
        limit=8 * 2**20 + 8 * held.size,
    )[0]


class Sum:
    def __init__(self, keep, send):
        self.keep, self.got, self.step = keep, swap(send), -1
        self.steps = lax.axis_size("batch").bit_length() - 1
        self.chunk = None

    def fold(self, last=BF, micros=0.4):
        if self.chunk is not None:
            return
        out = fold(self.keep, self.got, last, micros)
        self.step += 1
        if self.step == self.steps:
            self.chunk = out
        else:
            self.keep = out[1]
            self.got = hop(out[0], self.step)

    def finish(self, last=BF):
        while self.chunk is None:
            self.fold(last)
        return self.chunk


class Gather:
    def __init__(self, chunk, batch):
        self.held, self.other = chunk[None], None
        self.steps = list(reversed(range(batch.bit_length() - 1)))
        self.got = hop(self.held, self.steps[0])

    def join(self, plain=False, micros=0.4):
        if self.other is not None:
            return
        if plain:
            self.held = jnp.concatenate([self.held, self.got], axis=0)
        else:
            self.held = join(self.held, self.got, micros)
        self.steps.pop(0)
        if self.steps:
            self.got = hop(self.held, self.steps[0])
        else:
            self.other = swap(self.held)

    def finish(self, plain=False):
        while self.other is None:
            self.join(plain)
        return self.held, self.other


def share(chunk):
    return lax.all_gather(chunk, ("batch", "seq"), axis=0)


def mend_kernel(where, own_ref, other_ref, out_ref, *, seqs):
    ours = pl.program_id(0) // seqs == where[1]

    @pl.when(ours)
    def _():
        out_ref[...] = own_ref[...]

    @pl.when(jnp.logical_not(ours))
    def _():
        out_ref[...] = other_ref[...]


def mend(where, own, other):
    seqs, half_len, model = other.shape
    block = (1, half_len, model)
    return launch(
        functools.partial(mend_kernel, seqs=seqs),
        [own, other],
        [
            pl.BlockSpec(block, lambda i, w: (i % seqs, 0, 0)),
            pl.BlockSpec(block, lambda i, w: (i % seqs, 0, 0)),
        ],
        [pl.BlockSpec(block, lambda i, w: (i, 0, 0))],
        [jax.ShapeDtypeStruct((2 * seqs, half_len, model), BF)],
        (2 * seqs,),
        "mend",
        cost(6), limit=16 * 2**20,
        prefetch=[where],
    )[0]


def spread_kernel(in_ref, out_ref, *, flip):
    row_blocks, _, _, rows, cols = in_ref.shape
    block = in_ref[...].reshape(row_blocks * rows, cols).astype(F32)
    out_ref[...] = block.T if flip else block


def spread(gathered, batch, rows, cols, flip=False):
    row_blocks, chunk_rows, chunk_cols = chunk_shape(batch, rows, cols // 2)
    view = gathered.reshape(row_blocks, batch // row_blocks, 2, chunk_rows, chunk_cols)
    tw = next(size for size in (512, 384, 256, 128) if chunk_cols % size == 0)
    per, half = chunk_cols // tw, cols // 2 // tw
    return launch(
        functools.partial(spread_kernel, flip=flip),
        [view],
        [
            pl.BlockSpec(
                (row_blocks, 1, 1, chunk_rows, tw),
                lambda i: (0, (i % half) // per, i // half, 0, i % per),
            )
        ],
        [
            pl.BlockSpec((tw, rows), lambda i: (i, 0))
            if flip
            else pl.BlockSpec((rows, tw), lambda i: (0, i))
        ],
        [jax.ShapeDtypeStruct((cols, rows) if flip else (rows, cols), F32)],
        (cols // tw,),
        "spread",
        cost(8), limit=20 * 2**20,
    )[0]


def spread_near_kernel(where, own_ref, other_ref, *outs, steps, orders, row_blocks, splits):
    me, core = where[0], where[1]
    chunks, rows, tw = own_ref.shape
    col_blocks = chunks // row_blocks
    step = pl.program_id(0)
    block = (step % steps) * col_blocks // steps if col_blocks > 1 else 0
    tile = jnp.where(step < steps, core, 1 - core) * steps + step % steps

    def write(ref, half, out_ref):
        for row in range(row_blocks):
            owner = row * col_blocks + block
            spot = jnp.where(half == 0, place(owner, me, orders[0]), place(owner, me, orders[1]))
            out_ref[row * rows : (row + 1) * rows, :] = ref[spot].astype(F32)

    for ours in (True, False):
        for out_ref, first, last in zip(outs, splits[:-1], splits[1:]):

            @pl.when(
                jnp.logical_and((step < steps) == ours, jnp.logical_and(tile >= first, tile < last))
            )
            def _():
                if ours:
                    write(own_ref, core, out_ref)
                else:
                    write(other_ref, 1 - core, out_ref)


def spread_near(where, own, other, rows, widths):
    batch, chunk_rows, chunk_cols = own.shape
    row_blocks = rows // chunk_rows
    tw = next(size for size in (768, 512, 384, 256, 128) if chunk_cols % size == 0)
    steps, per = sum(widths) // 2 // tw, chunk_cols // tw
    splits = [sum(widths[:index]) // tw for index in range(len(widths) + 1)]
    tile = lambda i, w: jnp.where(i < steps, w[1], 1 - w[1]) * steps + i % steps

    def column(first, last):
        def pick(i, w):
            at = tile(i, w)
            idle = jnp.where(i < steps, 0, last - first - 1) if first else last - 1
            return (0, jnp.where(jnp.logical_and(at >= first, at < last), at - first, idle))

        return pick

    return launch(
        functools.partial(
            spread_near_kernel, steps=steps, orders=bit_orders(batch), row_blocks=row_blocks,
            splits=splits,
        ),
        [own, other],
        [
            pl.BlockSpec(
                (batch, chunk_rows, tw), lambda i, w: (0, 0, jnp.minimum(i, steps - 1) % per)
            ),
            pl.BlockSpec(
                (batch, chunk_rows, tw), lambda i, w: (0, 0, jnp.maximum(i - steps, 0) % per)
            ),
        ],
        [
            pl.BlockSpec((rows, tw), column(first, last))
            for first, last in zip(splits[:-1], splits[1:])
        ],
        [jax.ShapeDtypeStruct((rows, width), F32) for width in widths],
        (2 * steps,),
        "spread_near",
        cost(8), limit=24 * 2**20,
        prefetch=[where],
    )


def small_plan(rows, devices):
    each = -(-sum(rows) // devices // 16) * 16
    plan = [[] for _ in range(devices)]
    start = 0
    for source, count in enumerate(rows):
        done = 0
        while done < count:
            chunk, at = divmod(start + done, each)
            size = min(count - done, each - at)
            plan[chunk].append((source, done, at, size))
            done += size
        start += count
    return each, plan


def pack_kernel(
    where, buckets, gpos_ref, gwin_ref, ghead_ref, gtime_ref, ggain_a_ref, ggain_m_ref, gscale_ref,
    ids_ref, grows_ref, keep_ref, send_ref, extra_ref, *, each, plan, orders, buckets_in, span,
):
    me, core = where[0], where[1]
    batch = keep_ref.shape[0]
    panels = gpos_ref.shape[1] // 128
    extra_ref[...] = jnp.zeros_like(extra_ref)
    for seq in range(gtime_ref.shape[0]):
        extra_ref[pl.ds(buckets[core * gtime_ref.shape[0] + seq], 1), :] += gtime_ref[seq : seq + 1, :]
    extra_ref[buckets_in : buckets_in + 1, :] = ggain_a_ref[...]
    extra_ref[buckets_in + 1 : buckets_in + 2, :] = ggain_m_ref[...]
    extra_ref[buckets_in + 2 : buckets_in + 3, :128] = gscale_ref[...]
    sources = (gpos_ref, gwin_ref, ghead_ref, extra_ref)
    for chunk, pieces in enumerate(plan):
        half, owner = divmod(chunk, batch)
        spot = place(owner, me, orders[half])

        def write(ref):
            for panel in range(panels):
                base = panel * each
                filled = 0
                for source, first, at, size in pieces:
                    ref[spot, base + at : base + at + size, :] = sources[source][
                        first : first + size, panel * 128 : (panel + 1) * 128
                    ].astype(ref.dtype)
                    filled = at + size
                if filled < each:
                    ref[spot, base + filled : base + each, :] = jnp.zeros(
                        (each - filled, 128), ref.dtype
                    )

        @pl.when(core == half)
        def _():
            write(keep_ref)

        @pl.when(core != half)
        def _():
            write(send_ref)


    grows = grows_ref[...]
    per = min(4, batch)
    below = slice(panels * each, None)

    def gather_rows(index, _):
        start = index * per * 2 * span
        row = lax.broadcasted_iota(jnp.int32, (per * 2 * span, ids_ref.shape[1]), 0) + start
        one = jnp.where(row == ids_ref[...], 1.0, 0.0).astype(BF)
        sums = dot(one, grows)
        for owner in range(per):
            for half in range(2):
                part = sums[(owner * 2 + half) * span : (owner * 2 + half + 1) * span, :]
                spot = place(index * per + owner, me, orders[half])

                @pl.when(core == half)
                def _():
                    keep_ref[spot, below, :] = part

                @pl.when(core != half)
                def _():
                    send_ref[spot, below, :] = part.astype(BF)

        return 0

    lax.fori_loop(0, batch // per, gather_rows, 0)


def small_rows(length, width, bucket_count):
    return [length, width, width, -(-(bucket_count + 3) // 16) * 16]


def pack(
    where, buckets, gpos, gwin, ghead, gtime, ggain_a, ggain_m, gscale, ids, grows, batch, span,
    bucket_count,
):
    model, width = gpos.shape[1], gwin.shape[0]
    rows = small_rows(gpos.shape[0], width, bucket_count)
    each, plan = small_plan(rows, 2 * batch)
    shape = (batch, each * (model // 128) + span, 128)
    arrays = [gpos, gwin, ghead, gtime, ggain_a, ggain_m, gscale, ids, grows]
    return launch(
        functools.partial(
            pack_kernel, each=each, plan=plan, orders=bit_orders(batch), buckets_in=bucket_count,
            span=span,
        ),
        arrays,
        [whole(array.shape) for array in arrays],
        [whole(shape)] * 2,
        [jax.ShapeDtypeStruct(shape, F32), jax.ShapeDtypeStruct(shape, BF)],
        (1,),
        "pack_small",
        cost(12), limit=34 * 2**20,
        prefetch=[where, buckets],
        scratch=[pltpu.VMEM((rows[3], model), F32)],
    )


def unpack_kernel(
    where, own_ref, other_ref, mine_ref, table_ref, scal_ref,
    pos_ref, win_ref, head_ref, time_ref, gain_a_ref, gain_m_ref, gtable_ref, turned_ref, extra_ref,
    *, each, plan, orders, vocab,
):
    me, core = where[0], where[1]
    batch = own_ref.shape[0]
    panels = pos_ref.shape[1] // 128
    outs = (pos_ref, win_ref, turned_ref, extra_ref)
    for chunk, pieces in enumerate(plan):
        half, owner = divmod(chunk, batch)
        spot = place(owner, me, orders[half])

        def read(ref):
            for panel in range(panels):
                for source, first, at, size in pieces:
                    base = panel * each + at
                    outs[source][first : first + size, panel * 128 : (panel + 1) * 128] = ref[
                        spot, base : base + size, :
                    ].astype(F32)

        if pieces:

            @pl.when(core == half)
            def _():
                read(own_ref)

            @pl.when(core != half)
            def _():
                read(other_ref)

    head_ref[...] = turned_ref[...].T
    count, width = time_ref.shape[0], table_ref.shape[1]
    time_ref[...] = extra_ref[:count, :]
    gain_a_ref[...] = extra_ref[count, :]
    gain_m_ref[...] = extra_ref[count + 1, :]
    scale = jnp.sum(extra_ref[count + 2 : count + 3, :128], axis=1, keepdims=True)
    mean_norm = scal_ref[0:1, 4:5]
    grad_mean = -math.sqrt(width) / (mean_norm * mean_norm) * scale
    table = table_ref[...].astype(F32)
    norms = jnp.sqrt(jnp.sum(table * table, axis=1, keepdims=True) + 1e-06)
    gtable_ref[...] = mine_ref[: table.shape[0], :] + grad_mean / vocab * table / norms


def unpack(where, own, other, mine, table, scal, length, model, bucket_count, vocab):
    batch = own.shape[0]
    width = table.shape[1]
    rows = small_rows(length, width, bucket_count)
    each, plan = small_plan(rows, 2 * batch)
    shapes = [
        (length, model), (width, model), (model, width), (bucket_count, model), (model,), (model,),
        table.shape,
    ]
    arrays = [own, other, mine, table, scal]
    return launch(
        functools.partial(unpack_kernel, each=each, plan=plan, orders=bit_orders(batch), vocab=vocab),
        arrays,
        [whole(array.shape) for array in arrays],
        [whole(shape) for shape in shapes],
        [jax.ShapeDtypeStruct(shape, F32) for shape in shapes],
        (1,),
        "unpack_small",
        cost(5), limit=24 * 2**20,
        prefetch=[where],
        scratch=[pltpu.VMEM((width, model), F32), pltpu.VMEM((rows[3], model), F32)],
    )


def local(
    word_ids, buckets, noise, table, w_in, time_table, pos_table, gain_attn, w_qkv, w_out,
    gain_mlp, w_up, w_down, w_head,
):
    ORDER.clear()
    seq_rows, half_len = word_ids.shape
    table_span, embed_width = table.shape
    model = w_qkv.shape[0]
    bucket_count = time_table.shape[0]
    batch, cores = lax.axis_size("batch"), lax.axis_size("seq")
    devices = batch * cores
    vocab = table_span * devices
    length = half_len * cores
    seqs = seq_rows // cores
    tokens = seqs * length
    me = lax.axis_index("batch").astype(jnp.int32)
    core = lax.axis_index("seq").astype(jnp.int32)
    where = jnp.stack([me, core])

    def regroup(array):
        own = lax.dynamic_slice_in_dim(array, core * seqs, seqs, 0)
        other = swap(lax.dynamic_slice_in_dim(array, (1 - core) * seqs, seqs, 0))
        return jnp.concatenate(
            [jnp.where(core == 0, own, other), jnp.where(core == 0, other, own)], axis=1
        )

    bucket_hot = (buckets[:, None] == jnp.arange(bucket_count, dtype=jnp.int32)[None, :]).astype(F32)
    span = -(-(table_span + 1) // 16) * 16
    behind = jnp.pad(
        jnp.sum(bucket_hot, axis=0).astype(BF)[None, :],
        ((0, span - table_span - 1), (0, embed_width - bucket_count)),
    )
    own_table, other_table = Gather(jnp.concatenate([table, behind], axis=0), batch).finish(True)
    word_list = regroup(word_ids)
    device = lax.div(word_list, table_span)
    row_in = word_list - device * table_span
    owner, its_core = lax.div(device, cores), lax.rem(device, cores)
    orders = bit_orders(batch)
    spot = jnp.where(its_core == 0, place(owner, me, orders[0]), place(owner, me, orders[1]))
    spot = jnp.where(its_core == core, spot, spot + batch)
    ids = (spot * span + row_in).reshape(1, tokens)
    home = (device * span + row_in).reshape(1, tokens)
    noise_rows = regroup(noise).reshape(tokens, embed_width)

    word, noisy, stream, lefts, packed, scal = embed(
        buckets, ids, own_table, other_table, noise_rows, w_in, time_table, pos_table, gain_attn,
        w_qkv, table_span, where,
    )
    lefts, probs, inv = attend(packed, length, lefts)
    mid, mlp, act, slope, ours, theirs, gpred, branch, ghead = forward(
        where, scal, lefts, stream, word, w_out, gain_mlp, w_up, w_down, w_head, length
    )
    pairs = tokens // length * (packed.shape[1] // (6 * HEAD))
    inner = w_up.shape[1]

    def attend_part(first, last, grads):
        return attend_back(packed, gmixed, lefts, inv, probs, length, first, last - first, grads)

    (down,) = outer(where, branch[None], act[None], batch, 512, by_device=True)
    down_sum = lax.psum_scatter(
        down.reshape(devices, *down.shape[2:]), ("batch", "seq"), scatter_dimension=0, tiled=False
    )
    upin, gmid, grads, gmixed, ggain_m = back(
        mid, slope, gpred, branch, w_out, gain_mlp, w_up, w_down, w_head
    )
    sizes = [0, pairs // 3, pairs * 2 // 3, pairs]
    up = Sum(*outer(where, mlp[None], upin[None], batch, 512))
    for part in range(3):
        grads = attend_part(sizes[part], sizes[part + 1], grads)
        up.fold()
    attn = Sum(*outer(where, lefts, grads, batch))
    up.fold(micros=25)
    down_all = share(rounded(down_sum))
    attn.fold()
    up_all = Gather(up.finish(), batch)
    gpos, gtime, ggain_a, gwin, grows, gscale = input_back(
        scal, gmid, grads, stream, noisy, word, gpred, gain_attn, w_qkv, w_in, length
    )
    attn.fold()
    up_all.join()
    small = Sum(
        *pack(
            where, buckets, gpos, gwin, ghead, gtime, ggain_a, ggain_m, gscale, home, grows, batch,
            span, bucket_count,
        )
    )
    attn.fold()
    up_all.join(micros=25)
    small.fold(F32)
    output = mend(where, ours, swap(theirs))
    small.fold(F32)
    attn.fold()
    up_all.join()
    small.fold(F32)
    attn_all = Gather(attn.finish(), batch)
    grad_down = spread(down_all, batch, model, inner, True)
    attn_all.join()
    small.fold(F32)
    up_own, up_other = up_all.finish()
    mine = small.finish(F32)
    cut = mine.shape[0] - span
    small_all = Gather(mine[:cut].astype(BF), batch)
    attn_all.join()
    small_all.join()
    small_all.join()
    attn_all.join()
    (grad_up,) = spread_near(where, up_own, up_other, model, (inner,))
    small_all.join()
    attn_own, attn_other = attn_all.finish()
    small_own, small_other = small_all.finish()
    grad_qkv, grad_out = spread_near(where, attn_own, attn_other, model, (3 * model, model))
    pos_sum, win_sum, head_sum, time_sum, gain_a_sum, gain_m_sum, grad_table = unpack(
        where, small_own, small_other, mine[cut:], table, scal, length, model, bucket_count, vocab
    )
    return (
        output,
        grad_table,
        win_sum,
        time_sum,
        pos_sum,
        gain_a_sum,
        grad_qkv,
        grad_out,
        gain_m_sum,
        grad_up,
        grad_down,
        head_sum,
        scal[0, 4],
    )


def solution(mesh):
    rows = P(("batch", "seq"), None)
    in_specs = (P("batch", "seq"), P("batch"), P("batch", "seq", None), rows) + (P(),) * 10
    out_specs = (P("batch", "seq", None), rows) + (P(),) * 11
    return jax.shard_map(local, mesh=mesh, in_specs=in_specs, out_specs=out_specs, check_vma=False)
```

```python
import functools
import math

import jax
import jax.numpy as jnp
from jax import lax
from jax.experimental import pallas as pl
from jax.experimental.pallas import tpu as pltpu
from jax.sharding import PartitionSpec as P

HEAD = 64
BF = jnp.bfloat16
F32 = jnp.float32
NN = (((1,), (0,)), ((), ()))
NT = (((1,), (1,)), ((), ()))
TN = (((0,), (0,)), ((), ()))
VMEM_BYTES = 50 * 2**20
GELU_A = math.sqrt(2 / math.pi)
GELU_B = 0.044715


def dot(left, right, dims=NN):
    return lax.dot_general(left, right, dims, preferred_element_type=F32)


def params(limit=VMEM_BYTES):
    return pltpu.CompilerParams(vmem_limit_bytes=limit)


def cost(micros):
    return pl.CostEstimate(flops=int(micros * 1.2e9), bytes_accessed=0, transcendentals=0)


def whole(shape):
    return pl.BlockSpec(shape, lambda *_: (0,) * len(shape), pipeline_mode=pl.Buffered(1))


def smem():
    return pl.BlockSpec(memory_space=pltpu.SMEM)


def normalise(hidden):
    centre = hidden - jnp.mean(hidden, axis=-1, keepdims=True)
    inv = lax.rsqrt(jnp.mean(centre * centre, axis=-1, keepdims=True) + 1e-05)
    return centre * inv, inv


def norm_back(hidden, gain, grad):
    unit, inv = normalise(hidden)
    scaled = grad * gain
    part = inv * (
        scaled
        - jnp.mean(scaled, axis=-1, keepdims=True)
        - unit * jnp.mean(scaled * unit, axis=-1, keepdims=True)
    )
    return part, jnp.sum(grad * unit, axis=0, keepdims=True)


ORDER = []


def launch(kernel, inputs, in_specs, out_specs, out_shape, grid, name, estimate, prefetch=(), aliases=None, scratch=(), limit=VMEM_BYTES, chained=True):
    count = len(prefetch) + len(inputs)
    outs, waits = len(out_shape), len(ORDER)

    def body(*refs):
        at = count + waits
        refs[at + outs][...] = jnp.zeros((8, 128), F32)
        kernel(*refs[:count], *refs[at : at + outs], *refs[at + outs + 1 :])

    token = pl.BlockSpec((8, 128), lambda *_: (0, 0)) if grid else resident(1)[0]
    *results, last = pl.pallas_call(
        body,
        grid_spec=pltpu.PrefetchScalarGridSpec(
            num_scalar_prefetch=len(prefetch),
            grid=grid,
            in_specs=list(in_specs) + anywhere(waits),
            out_specs=list(out_specs) + [token],
            scratch_shapes=list(scratch),
        ),
        out_shape=list(out_shape) + [jax.ShapeDtypeStruct((8, 128), F32)],
        input_output_aliases={len(prefetch) + k: v for k, v in (aliases or {}).items()},
        compiler_params=params(limit),
        cost_estimate=estimate,
        name=name,
    )(*prefetch, *inputs, *ORDER)
    if chained:
        ORDER[:] = [last]
    return results


def resident(count):
    return [pl.BlockSpec(memory_space=pltpu.VMEM)] * count


def anywhere(count):
    return [pl.BlockSpec(memory_space=pl.ANY)] * count


def ignoring(kernel, inputs, extra):
    return lambda *refs: kernel(*refs[:inputs], *refs[inputs + extra :])


def accumulate(ref, first, value):
    @pl.when(first)
    def _():
        ref[...] = value

    @pl.when(jnp.logical_not(first))
    def _():
        ref[...] += value


def embed_kernel(
    where, buckets, ids_ref, own_ref, other_ref, noise_ref, win_ref, time_ref, pos_ref, gain_ref, wqkv_ref,
    word_ref, noisy_ref, stream_ref, left_ref, packed_ref, scal_ref, table_ref,
    *, tiles, table_span, seqs, step,
):
    index = pl.program_id(0)
    seq = index // tiles
    first = where[1] * seqs
    chunks, span, width = own_ref.shape
    bucket_count = time_ref.shape[0]

    @pl.when(index == 0)
    def _():
        real = lax.broadcasted_iota(jnp.int32, (span, 1), 0) < table_span
        norms = jnp.zeros((span, 1), F32)
        counts = jnp.zeros((1, width), F32)
        for half, ref in enumerate((own_ref, other_ref)):
            for chunk in range(chunks):
                block = ref[chunk].astype(F32)
                norms += jnp.where(
                    real, jnp.sqrt(jnp.sum(block * block, axis=1, keepdims=True) + 1e-06), 0.0
                )
                counts += block[table_span : table_span + 1, :]
                at = (half * chunks + chunk) * span
                table_ref[:, at : at + span] = block.T.astype(BF)
        mean_norm = jnp.sum(norms, axis=0, keepdims=True) / (2 * chunks * table_span)
        lane = lax.broadcasted_iota(jnp.int32, (1, width), 1)
        scal_ref[...] = jnp.zeros_like(scal_ref)
        for each in range(seqs):
            bucket = buckets[first + each]
            signal, spread = jnp.float32(0.0), jnp.float32(0.0)
            for kind in range(bucket_count):
                angle = math.pi / 2 * (kind + 1.0) / (bucket_count + 1)
                signal = jnp.where(bucket == kind, math.cos(angle), signal)
                spread = jnp.where(bucket == kind, math.sin(angle), spread)
            count = jnp.sum(jnp.where(lane == bucket, counts, 0.0), axis=1, keepdims=True)
            row = jnp.where(lane == 0, signal, jnp.where(lane == 1, spread, 0.0))
            row = jnp.where(lane == 2, 2.0 / count, row)
            row = jnp.where(lane == 3, math.sqrt(width) / mean_norm, row)
            scal_ref[each : each + 1, :] = jnp.where(lane == 4, mean_norm, row)

    ids = ids_ref[...]
    word = jnp.zeros((width, ids.shape[1]), F32)
    for start in range(0, 2 * chunks * span, step):
        row = lax.broadcasted_iota(jnp.int32, (step, ids.shape[1]), 0) + start
        one = jnp.where(row == ids, 1.0, 0.0).astype(BF)
        word += dot(table_ref[:, start : start + step], one)
    word = word.T
    word_ref[...] = word.astype(BF)
    scal = scal_ref[pl.ds(seq, 1), :]
    clean = word * scal[:, 3:4]
    noisy = (scal[:, 0:1] * clean + scal[:, 1:2] * noise_ref[...].astype(F32)).astype(BF)
    noisy_ref[...] = noisy
    stream = dot(noisy, win_ref[...]) + time_ref[pl.ds(buckets[first + seq], 1), :] + pos_ref[...]
    stream_ref[...] = stream
    attn = (normalise(stream)[0] * gain_ref[...].reshape(1, -1)).astype(BF)
    left_ref[0] = attn
    packed_ref[...] = dot(attn, wqkv_ref[...]).astype(BF)


def embed(buckets, ids, own, other, noise, w_in, time_table, pos_table, gain, w_qkv, table_span, where, tm=256):
    tokens, width = noise.shape
    length, model = pos_table.shape
    seqs, tiles = tokens // length, length // tm
    wide = w_qkv.shape[1]
    rows = 2 * own.shape[0] * own.shape[1]
    row = lambda cols: pl.BlockSpec((tm, cols), lambda i, *_: (i, 0))
    return launch(
        functools.partial(
            embed_kernel, tiles=tiles, table_span=table_span, seqs=seqs, step=min(rows, 1024)
        ),
        [ids, own, other, noise, w_in, time_table, pos_table, gain, w_qkv],
        [
            pl.BlockSpec((1, tm), lambda i, *_: (0, i)), whole(own.shape), whole(other.shape),
            row(width), whole(w_in.shape), whole(time_table.shape),
            pl.BlockSpec((tm, model), lambda i, *_: (i % tiles, 0)), whole(gain.shape),
            whole(w_qkv.shape),
        ],
        [
            row(width), row(width), row(model), pl.BlockSpec((1, tm, model), lambda i, *_: (0, i, 0)),
            row(wide), pl.BlockSpec((8, width), lambda *_: (0, 0)),
        ],
        [
            jax.ShapeDtypeStruct((tokens, width), BF),
            jax.ShapeDtypeStruct((tokens, width), BF),
            jax.ShapeDtypeStruct((tokens, model), F32),
            jax.ShapeDtypeStruct((2, tokens, model), BF),
            jax.ShapeDtypeStruct((tokens, wide), BF),
            jax.ShapeDtypeStruct((8, width), F32),
        ],
        (tokens // tm,),
        "embed",
        cost(tokens / 80),
        prefetch=[where, buckets],
        scratch=[pltpu.VMEM((width, rows), BF)],
    )


def attend_kernel(q_ref, k_ref, v_ref, mixed_ref, probs_ref, inv_ref, *, tq):
    length = q_ref.shape[0]
    lane = lax.broadcasted_iota(jnp.int32, (1, 2 * HEAD), 1)
    keys = k_ref[...]
    values = jnp.concatenate([v_ref[...], jnp.ones_like(v_ref[...])], axis=1)
    scale = math.log2(math.e) * HEAD**-0.5
    for start in range(0, length, tq):
        rows = slice(start, start + tq)
        query = q_ref[rows, :]
        parts = []
        for head in range(2):
            own = jnp.where(lane // HEAD == head, query, jnp.zeros_like(query))
            scores = dot(own, keys, NT)
            peak = jnp.max(scores, axis=1, keepdims=True)
            raised = jnp.exp2(scores * scale - peak * scale).astype(BF)
            probs_ref[head, rows, :] = raised
            sums = dot(raised, values)
            inv = 1.0 / sums[:, 2 * HEAD :]
            parts.append((sums[:, : 2 * HEAD] * inv, inv))
        low = lane < HEAD
        mixed_ref[0, rows, :] = jnp.where(low, parts[0][0], parts[1][0]).astype(BF)
        inv_ref[rows, :] = jnp.where(low, parts[0][1], parts[1][1])


def attend(packed, length, lefts, tq=256):
    tokens = packed.shape[0]
    seqs, pairs = tokens // length, packed.shape[1] // (6 * HEAD)
    spec = lambda part: pl.BlockSpec((length, 2 * HEAD), lambda s, j: (s, part * pairs + j))
    return launch(
        ignoring(functools.partial(attend_kernel, tq=tq), 3, 1),
        [packed, packed, packed, lefts],
        [spec(0), spec(1), spec(2)] + anywhere(1),
        [
            pl.BlockSpec((1, length, 2 * HEAD), lambda s, j: (1, s, j)),
            pl.BlockSpec((2, length, length), lambda s, j: (s * pairs + j, 0, 0)), spec(0),
        ],
        [
            jax.ShapeDtypeStruct(lefts.shape, BF),
            jax.ShapeDtypeStruct((seqs * pairs * 2, length, length), BF),
            jax.ShapeDtypeStruct((tokens, pairs * 2 * HEAD), F32),
        ],
        (seqs, pairs),
        "attend",
        cost(3.5 * seqs * pairs),
        aliases={3: 0},
    )


def attend_back_kernel(
    q_ref, k_ref, v_ref, grad_ref, mixed_ref, inv_ref, probs_ref, out_ref, *, tq
):
    length = q_ref.shape[0]
    lane = lax.broadcasted_iota(jnp.int32, (1, 2 * HEAD), 1)
    keys, values = k_ref[...], v_ref[...]
    scale = HEAD**-0.5
    held = [None] * (length // tq)
    key_parts, value_parts = [], []
    for head in range(2):
        mask = lane // HEAD == head
        grad_k, grad_v = None, None
        cut = slice(head * HEAD, (head + 1) * HEAD)
        for tile in range(length // tq):
            rows = slice(tile * tq, (tile + 1) * tq)
            grad = grad_ref[rows, :]
            inv = inv_ref[rows, :]
            wide = grad.astype(F32)
            inner = jnp.sum(
                jnp.where(mask, wide * mixed_ref[0, rows, :].astype(F32), 0.0), axis=1, keepdims=True
            )
            grad_probs = dot(jnp.where(mask, grad, jnp.zeros_like(grad)), values, NT)
            raised = probs_ref[head, rows, :]
            grad_scores = (raised.astype(F32) * (grad_probs - inner)).astype(BF)
            grad_q = dot(grad_scores, keys) * (inv * scale)
            if head == 0:
                held[tile] = grad_q
            else:
                out_ref[0, rows, :] = jnp.where(lane < HEAD, held[tile], grad_q).astype(BF)
            query = (q_ref[rows, :].astype(F32) * (inv * scale)).T[cut, :].astype(BF)
            outer = (wide * inv).T[cut, :].astype(BF)
            part_k, part_v = dot(query, grad_scores), dot(outer, raised)
            grad_k = part_k if grad_k is None else grad_k + part_k
            grad_v = part_v if grad_v is None else grad_v + part_v
        key_parts.append(grad_k)
        value_parts.append(grad_v)
    out_ref[1] = jnp.concatenate(key_parts, axis=0).T.astype(BF)
    out_ref[2] = jnp.concatenate(value_parts, axis=0).T.astype(BF)


def attend_back(packed, grad_mixed, lefts, inv, probs, length, first, count, held, tq=256):
    pairs = packed.shape[1] // (6 * HEAD)
    at = lambda i: ((first + i) // pairs, (first + i) % pairs)
    spec = lambda part: pl.BlockSpec(
        (length, 2 * HEAD), lambda i: (at(i)[0], part * pairs + at(i)[1])
    )
    return launch(
        ignoring(functools.partial(attend_back_kernel, tq=tq), 7, 1),
        [packed, packed, packed, grad_mixed, lefts, inv, probs, held],
        [
            spec(0), spec(1), spec(2), spec(0),
            pl.BlockSpec((1, length, 2 * HEAD), lambda i: (1, *at(i))), spec(0),
            pl.BlockSpec((2, length, length), lambda i: (first + i, 0, 0)),
        ]
        + anywhere(1),
        [pl.BlockSpec((3, length, 2 * HEAD), lambda i: (0, *at(i)))],
        [jax.ShapeDtypeStruct(held.shape, BF)],
        (count,),
        "attend_back",
        cost(4.5 * count), limit=34 * 2**20,
        aliases={7: 0},
    )[0]


def forward_kernel(
    where, scal_ref, mixed_ref, stream_ref, word_ref, wout_ref, gain_ref, wup_ref, wdown_ref, whead_ref,
    mid_ref, mlp_ref, act_ref, slope_ref, ours_ref, theirs_ref, gpred_ref, branch_ref, ghead_ref,
    *, tiles, step,
):
    index = pl.program_id(0)
    seq = index // tiles
    mid = stream_ref[...] + dot(mixed_ref[0], wout_ref[...])
    mid_ref[...] = mid
    mlp = (normalise(mid)[0] * gain_ref[...].reshape(1, -1)).astype(BF)
    mlp_ref[...] = mlp
    total = mid
    for start in range(0, wup_ref.shape[1], step):
        cols = slice(start, start + step)
        up = dot(mlp, wup_ref[:, cols])
        inner = (2.0 * GELU_A * GELU_B) * (up * up) + 2.0 * GELU_A
        share = 0.5 + 0.5 * jnp.tanh(up * (0.5 * inner))
        full = up * share
        act = full.astype(BF)
        act_ref[:, cols] = act
        slope = share + full * (1.0 - share) * (3.0 * inner - 4.0 * GELU_A)
        slope_ref[:, cols] = slope.astype(BF)
        total = total + dot(act, wdown_ref[cols, :])
    low = total.astype(BF)
    half = (index % tiles) // (tiles // 2)

    @pl.when(half == where[1])
    def _():
        ours_ref[0] = low

    @pl.when(half != where[1])
    def _():
        theirs_ref[0] = low

    scal = scal_ref[pl.ds(seq, 1), :]
    clean = word_ref[...].astype(F32) * scal[:, 3:4]
    gpred = (dot(low, whead_ref[...]) - clean) * scal[:, 2:3]
    gpred_ref[...] = gpred
    gpred_low = gpred.astype(BF)
    branch_ref[...] = dot(gpred_low, whead_ref[...], NT).astype(BF)
    accumulate(ghead_ref, index == 0, dot(gpred.T.astype(BF), low))


def forward(where, scal, lefts, stream, word, w_out, gain, w_up, w_down, w_head, length, tm=256, step=768):
    tokens, model = stream.shape
    inner, width = w_up.shape[1], w_head.shape[1]
    row = lambda cols: pl.BlockSpec((tm, cols), lambda i, *_: (i, 0))
    shape = lambda cols, kind: jax.ShapeDtypeStruct((tokens, cols), kind)
    tiles = length // tm
    turn = lambda i, core: (i // tiles, jnp.clip(i % tiles - core * (tiles // 2), 0, tiles // 2 - 1), 0)
    halves = jax.ShapeDtypeStruct((tokens // length, length // 2, model), BF)
    return launch(
        functools.partial(forward_kernel, tiles=tiles, step=step),
        [scal, lefts, stream, word, w_out, gain, w_up, w_down, w_head],
        [
            whole(scal.shape), pl.BlockSpec((1, tm, model), lambda i, *_: (1, i, 0)), row(model), row(width),
            whole(w_out.shape), whole(gain.shape), whole(w_up.shape), whole(w_down.shape),
            whole(w_head.shape),
        ],
        [
            row(model), row(model), row(inner), row(inner),
            pl.BlockSpec((1, tm, model), lambda i, w: turn(i, w[1])),
            pl.BlockSpec((1, tm, model), lambda i, w: turn(i, 1 - w[1])), row(width), row(model),
            pl.BlockSpec((width, model), lambda *_: (0, 0)),
        ],
        [
            shape(model, F32), shape(model, BF), shape(inner, BF), shape(inner, BF),
            halves, halves, shape(width, F32), shape(model, BF),
            jax.ShapeDtypeStruct((width, model), F32),
        ],
        (tokens // tm,),
        "feed_forward",
        cost(tokens / 45),
        prefetch=[where],
    )


def back_kernel(
    mid_ref, slope_ref, gpred_ref, branch_ref, wout_ref, gain_ref, wup_ref, wdown_ref, whead_ref,
    upin_ref, gmid_ref, gattn_ref, gmixed_ref, ggain_ref, *, step,
):
    index = pl.program_id(0)
    branch = branch_ref[...]
    grad = None
    for start in range(0, wup_ref.shape[1], step):
        cols = slice(start, start + step)
        upin = (dot(branch, wdown_ref[cols, :], NT) * slope_ref[:, cols].astype(F32)).astype(BF)
        upin_ref[:, cols] = upin
        part = dot(upin, wup_ref[:, cols], NT)
        grad = part if grad is None else grad + part
    part, gain_part = norm_back(mid_ref[...], gain_ref[...].reshape(1, -1), grad)
    accumulate(ggain_ref, index == 0, gain_part)
    gmid = dot(gpred_ref[...].astype(BF), whead_ref[...], NT) + part
    gmid_ref[...] = gmid
    low = gmid.astype(BF)
    gattn_ref[0] = low
    gmixed_ref[...] = dot(low, wout_ref[...], NT).astype(BF)


def back(mid, slope, gpred, branch, w_out, gain, w_up, w_down, w_head, tm=256, step=768):
    tokens, model = mid.shape
    inner, width = w_up.shape[1], w_head.shape[1]
    row = lambda cols: pl.BlockSpec((tm, cols), lambda i: (i, 0))
    shape = lambda cols, kind: jax.ShapeDtypeStruct((tokens, cols), kind)
    return launch(
        functools.partial(back_kernel, step=step),
        [mid, slope, gpred, branch, w_out, gain, w_up, w_down, w_head],
        [
            row(model), row(inner), row(width), row(model), whole(w_out.shape), whole(gain.shape),
            whole(w_up.shape), whole(w_down.shape), whole(w_head.shape),
        ],
        [
            row(inner), row(model), pl.BlockSpec((1, tm, model), lambda i: (3, i, 0)), row(model),
            pl.BlockSpec((1, model), lambda i: (0, 0)),
        ],
        [
            shape(inner, BF), shape(model, F32), jax.ShapeDtypeStruct((4, tokens, model), BF),
            shape(model, BF), jax.ShapeDtypeStruct((1, model), F32),
        ],
        (tokens // tm,),
        "feed_forward_back",
        cost(tokens / 55),
    )


def input_back_kernel(
    scal_ref, gmid_ref, dq_ref, dk_ref, dv_ref, stream_ref, noisy_ref, word_ref, gpred_ref, gain_ref,
    wqkv_ref, win_ref, gpos_ref, gtime_ref, ggain_ref, gwin_ref, grows_ref, gscale_ref,
):
    tile, seq = pl.program_id(0), pl.program_id(1)
    first = jnp.logical_and(tile == 0, seq == 0)
    model = win_ref.shape[1]
    grad = (
        dot(dq_ref[0], wqkv_ref[:, :model], NT)
        + dot(dk_ref[0], wqkv_ref[:, model : 2 * model], NT)
        + dot(dv_ref[0], wqkv_ref[:, 2 * model :], NT)
    )
    part, gain_part = norm_back(stream_ref[...], gain_ref[...].reshape(1, -1), grad)
    accumulate(ggain_ref, first, gain_part)
    gin = gmid_ref[...] + part
    accumulate(gpos_ref, seq == 0, gin)
    sums = jnp.sum(gin, axis=0, keepdims=True)
    @pl.when(tile == 0)
    def _():
        gtime_ref[pl.ds(seq, 1), :] = sums

    @pl.when(tile > 0)
    def _():
        gtime_ref[pl.ds(seq, 1), :] += sums

    low = gin.astype(BF)
    accumulate(gwin_ref, first, dot(noisy_ref[...].astype(F32).T.astype(BF), low))
    scal = scal_ref[pl.ds(seq, 1), :]
    gclean = scal[:, 0:1] * dot(low, win_ref[...], NT) - gpred_ref[...]
    grows_ref[...] = (gclean * scal[:, 3:4]).astype(BF)
    accumulate(
        gscale_ref, first, jnp.sum(word_ref[...].astype(F32) * gclean, axis=0, keepdims=True)
    )


def input_back(scal, gmid, grads, stream, noisy, word, gpred, gain, w_qkv, w_in, length, tm=256):
    tokens, model = gmid.shape
    width = w_in.shape[0]
    seqs, tiles = tokens // length, length // tm
    row = lambda cols: pl.BlockSpec((tm, cols), lambda i, s: (s * tiles + i, 0))
    plane = lambda part: pl.BlockSpec((1, tm, model), lambda i, s: (part, s * tiles + i, 0))
    fixed = lambda rows, cols: pl.BlockSpec((rows, cols), lambda i, s: (0, 0))
    return launch(
        input_back_kernel,
        [scal, gmid, grads, grads, grads, stream, noisy, word, gpred, gain, w_qkv, w_in],
        [
            whole(scal.shape), row(model), plane(0), plane(1), plane(2), row(model), row(width),
            row(width), row(width), whole(gain.shape), whole(w_qkv.shape), whole(w_in.shape),
        ],
        [
            pl.BlockSpec((tm, model), lambda i, s: (i, 0)), fixed(seqs, model), fixed(1, model),
            fixed(width, model), row(width), fixed(1, width),
        ],
        [
            jax.ShapeDtypeStruct((length, model), F32),
            jax.ShapeDtypeStruct((seqs, model), F32),
            jax.ShapeDtypeStruct((1, model), F32),
            jax.ShapeDtypeStruct((width, model), F32),
            jax.ShapeDtypeStruct((tokens, width), BF),
            jax.ShapeDtypeStruct((1, width), F32),
        ],
        (tiles, seqs),
        "input_back",
        cost(tokens / 90), limit=60 * 2**20,
    )


def bit_orders(batch):
    bits = list(range(batch.bit_length() - 1))
    return bits, bits[1:3] + bits[:1] + bits[3:]


def place(owner, me, order):
    apart = jnp.bitwise_xor(owner, me)
    spot = 0
    for bit in order:
        spot = spot * 2 + jnp.bitwise_and(lax.shift_right_logical(apart, bit), 1)
    return spot


def chunk_shape(batch, rows, cols):
    row_blocks = min(batch, 16 if batch <= 16 else 32)
    return row_blocks, rows // row_blocks, cols * row_blocks // batch


def outer_kernel(where, left_ref, right_ref, *outs, orders, row_blocks, tw, steps):
    me, core = where[0], where[1]
    acc = dot(left_ref[0], right_ref[0], TN)
    if len(outs) == 1:
        rows = outs[0].shape[2]
        for row in range(row_blocks):
            outs[0][row, 0] = acc[row * rows : (row + 1) * rows, :]
        return
    chunks, rows, cols = outs[0].shape
    col_blocks = chunks // row_blocks
    tile, per = pl.program_id(0), cols // tw
    half, step = tile // steps, tile % steps
    block = step // per if col_blocks > 1 else 0
    cut = pl.ds(pl.multiple_of((step % per) * tw, 128), tw) if col_blocks > 1 else slice(None)

    def write(ref):
        for row in range(row_blocks):
            owner = row * col_blocks + block
            spot = jnp.where(half == 0, place(owner, me, orders[0]), place(owner, me, orders[1]))
            ref[spot, :, cut] = acc[row * rows : (row + 1) * rows, :].astype(ref.dtype)

    @pl.when(core == half)
    def _():
        write(outs[0])

    @pl.when(core != half)
    def _():
        write(outs[1])


def outer(where, lefts, rights, batch, tw=768, by_device=False):
    _, tokens, rows = lefts.shape
    planes, _, width = rights.shape
    cols = planes * width
    row_blocks, chunk_rows, chunk_cols = chunk_shape(batch, rows, cols // 2)
    col_blocks = batch // row_blocks
    tw = next(size for size in (tw, 384, 256, 128) if chunk_cols % size == 0 and width % size == 0)
    per, steps, inside = width // tw, cols // 2 // tw, chunk_cols // tw
    left = lambda i, w: (jnp.where(i // per == planes - 1, lefts.shape[0] - 1, 0), 0, 0)
    if by_device:
        shapes = [jax.ShapeDtypeStruct((row_blocks, col_blocks * 2, chunk_rows, chunk_cols), F32)]
        at = lambda i, w: (0, (i % steps) // inside * 2 + i // steps, 0, i % inside)
        specs = [pl.BlockSpec((row_blocks, 1, chunk_rows, tw), at)]
    else:
        shape = (batch, chunk_rows, chunk_cols)
        shapes = [jax.ShapeDtypeStruct(shape, BF)] * 2
        early = lambda i: jnp.minimum(i, steps - 1)
        late = lambda i: jnp.maximum(i - steps, 0)
        specs = [
            pl.BlockSpec(
                (batch, chunk_rows, tw), lambda i, w: (0, 0, jnp.where(w[1] == 0, early(i), late(i)))
            ),
            pl.BlockSpec(
                (batch, chunk_rows, tw), lambda i, w: (0, 0, jnp.where(w[1] == 0, late(i), early(i)))
            ),
        ]
        if col_blocks > 1:
            specs = [whole(shape)] * 2
    return launch(
        functools.partial(
            outer_kernel, orders=bit_orders(batch), row_blocks=row_blocks, tw=tw, steps=steps
        ),
        [lefts, rights],
        [
            pl.BlockSpec((1, tokens, rows), left),
            pl.BlockSpec((1, tokens, tw), lambda i, w: (i // per, 0, i % per)),
        ],
        specs,
        shapes,
        (cols // tw,),
        "weight_grad",
        cost(tokens / 120),
        prefetch=[where],
    )


def swap(array):
    return lax.ppermute(array, "seq", [(0, 1), (1, 0)])


def hop(array, step):
    batch = lax.axis_size("batch")
    orders = bit_orders(batch)
    pairs = [
        (2 * me + core, 2 * (me ^ (1 << orders[core][step])) + core)
        for me in range(batch)
        for core in range(2)
    ]
    return lax.ppermute(array, ("batch", "seq"), pairs)


def fold_kernel(keep_ref, got_ref, *outs):
    count = keep_ref.shape[0] // 2
    if not count:
        outs[0][...] = (keep_ref[0] + got_ref[0].astype(F32)).astype(outs[0].dtype)
        return
    outs[0][...] = (keep_ref[count:] + got_ref[count:].astype(F32)).astype(BF)
    outs[1][...] = keep_ref[:count] + got_ref[:count].astype(F32)


def fold(keep, got, last=BF, micros=0.4, chained=True):
    count, tail = keep.shape[0] // 2, keep.shape[1:]
    if count:
        shapes = [jax.ShapeDtypeStruct((count, *tail), BF), jax.ShapeDtypeStruct((count, *tail), F32)]
    else:
        shapes = [jax.ShapeDtypeStruct(tail, last)]
    out = launch(
        fold_kernel, [keep, got], resident(2), resident(len(shapes)), shapes, (), "fold", cost(micros),
        limit=8 * 2**20 + 12 * keep.size, chained=chained,
    )
    return out if count else out[0]


def both_kernel(keep_ref, got_ref, other_ref, out_ref):
    out_ref[0] = other_ref[...].astype(BF)
    out_ref[1] = (keep_ref[0] + got_ref[0].astype(F32)).astype(BF)


def join_kernel(held_ref, got_ref, out_ref):
    count = held_ref.shape[0]
    out_ref[:count] = held_ref[...]
    out_ref[count:] = got_ref[...]


def join(held, got, micros):
    shape = (2 * held.shape[0], *held.shape[1:])
    return launch(
        join_kernel, [held, got], resident(2), resident(1),
        [jax.ShapeDtypeStruct(shape, held.dtype)], (), "join", cost(micros),
        limit=8 * 2**20 + 8 * held.size,
    )[0]


class Sum:
    def __init__(self, keep, send):
        self.keep, self.got, self.step = keep, swap(send), -1
        self.steps = lax.axis_size("batch").bit_length() - 1
        self.chunk = None

    def fold(self, last=BF, micros=0.4):
        if self.chunk is not None:
            return
        out = fold(self.keep, self.got, last, micros)
        self.step += 1
        if self.step == self.steps:
            self.chunk = out
        else:
            self.keep = out[1]
            self.got = hop(out[0], self.step)

    def finish_with(self, other):
        while self.step < self.steps - 1:
            self.fold()
        shape = jax.ShapeDtypeStruct((2, *other.shape), BF)
        return launch(
            both_kernel, [self.keep, self.got, other],
            [whole(self.keep.shape), whole(self.got.shape), whole(other.shape)], [whole(shape.shape)],
            [shape], (1,), "both", cost(0.4), limit=60 * 2**20,
        )[0]

    def finish(self, last=BF):
        while self.chunk is None:
            self.fold(last)
        return self.chunk


class Gather:
    def __init__(self, chunk, batch):
        self.held, self.other = chunk[None], None
        self.steps = list(reversed(range(batch.bit_length() - 1)))
        self.got = hop(self.held, self.steps[0])

    def join(self, plain=False, micros=0.4):
        if self.other is not None:
            return
        if plain:
            self.held = jnp.concatenate([self.held, self.got], axis=0)
        else:
            self.held = join(self.held, self.got, micros)
        self.steps.pop(0)
        if self.steps:
            self.got = hop(self.held, self.steps[0])
        else:
            self.other = swap(self.held)

    def finish(self, plain=False):
        while self.other is None:
            self.join(plain)
        return self.held, self.other


def mend_kernel(where, own_ref, other_ref, out_ref, *, seqs):
    ours = pl.program_id(0) // seqs == where[1]

    @pl.when(ours)
    def _():
        out_ref[...] = own_ref[...]

    @pl.when(jnp.logical_not(ours))
    def _():
        out_ref[...] = other_ref[...]


def mend(where, own, other):
    seqs, half_len, model = other.shape
    block = (1, half_len, model)
    return launch(
        functools.partial(mend_kernel, seqs=seqs),
        [own, other],
        [
            pl.BlockSpec(block, lambda i, w: (i % seqs, 0, 0)),
            pl.BlockSpec(block, lambda i, w: (i % seqs, 0, 0)),
        ],
        [pl.BlockSpec(block, lambda i, w: (i, 0, 0))],
        [jax.ShapeDtypeStruct((2 * seqs, half_len, model), BF)],
        (2 * seqs,),
        "mend",
        cost(6), limit=16 * 2**20,
        prefetch=[where],
    )[0]


def spread_near_kernel(where, own_ref, other_ref, *outs, steps, orders, row_blocks, splits, flip):
    me, core = where[0], where[1]
    *outs, whole_ref = outs
    chunks, _, rows, tw = own_ref.shape
    col_blocks = chunks // row_blocks
    step = pl.program_id(0)
    block = (step % steps) * col_blocks // steps if col_blocks > 1 else 0
    tile = jnp.where(step < steps, core, 1 - core) * steps + step % steps

    def write(ref, half, out_ref):
        for row in range(row_blocks):
            owner = row * col_blocks + block
            spot = jnp.where(half == 0, place(owner, me, orders[0]), place(owner, me, orders[1]))
            target = whole_ref if flip else out_ref
            target[row * rows : (row + 1) * rows, :] = ref[spot, 0].astype(F32)
        if flip:
            out_ref[...] = whole_ref[...].T

    for ours in (True, False):
        for out_ref, first, last in zip(outs, splits[:-1], splits[1:]):

            @pl.when(
                jnp.logical_and((step < steps) == ours, jnp.logical_and(tile >= first, tile < last))
            )
            def _():
                if ours:
                    write(own_ref, core, out_ref)
                else:
                    write(other_ref, 1 - core, out_ref)


def spread_near(where, own, other, which, rows, widths, flip=False):
    batch, _, chunk_rows, chunk_cols = own.shape
    row_blocks = rows // chunk_rows
    tw = next(size for size in (768, 512, 384, 256, 128) if chunk_cols % size == 0)
    steps, per = sum(widths) // 2 // tw, chunk_cols // tw
    splits = [sum(widths[:index]) // tw for index in range(len(widths) + 1)]
    tile = lambda i, w: jnp.where(i < steps, w[1], 1 - w[1]) * steps + i % steps

    def column(first, last):
        def pick(i, w):
            at = tile(i, w)
            idle = jnp.where(i < steps, 0, last - first - 1) if first else last - 1
            block = jnp.where(jnp.logical_and(at >= first, at < last), at - first, idle)
            return (block, 0) if flip else (0, block)

        return pick

    return launch(
        functools.partial(
            spread_near_kernel, steps=steps, orders=bit_orders(batch), row_blocks=row_blocks,
            splits=splits, flip=flip,
        ),
        [own, other],
        [
            pl.BlockSpec(
                (batch, 1, chunk_rows, tw),
                lambda i, w: (0, which, 0, jnp.minimum(i, steps - 1) % per),
            ),
            pl.BlockSpec(
                (batch, 1, chunk_rows, tw),
                lambda i, w: (0, which, 0, jnp.maximum(i - steps, 0) % per),
            ),
        ],
        [
            pl.BlockSpec((tw, rows) if flip else (rows, tw), column(first, last))
            for first, last in zip(splits[:-1], splits[1:])
        ],
        [jax.ShapeDtypeStruct((width, rows) if flip else (rows, width), F32) for width in widths],
        (2 * steps,),
        "spread_near",
        cost(8), limit=24 * 2**20,
        prefetch=[where],
        scratch=[pltpu.VMEM((rows, tw) if flip else (8, 128), F32)],
    )


def small_plan(rows, devices):
    each = -(-sum(rows) // devices // 16) * 16
    plan = [[] for _ in range(devices)]
    start = 0
    for source, count in enumerate(rows):
        done = 0
        while done < count:
            chunk, at = divmod(start + done, each)
            size = min(count - done, each - at)
            plan[chunk].append((source, done, at, size))
            done += size
        start += count
    return each, plan


def pack_kernel(
    where, buckets, gpos_ref, gwin_ref, ghead_ref, gtime_ref, ggain_a_ref, ggain_m_ref, gscale_ref,
    ids_ref, grows_ref, keep_ref, send_ref, extra_ref, *, each, plan, orders, buckets_in, span,
):
    me, core = where[0], where[1]
    batch = keep_ref.shape[0]
    panels = gpos_ref.shape[1] // 128
    extra_ref[...] = jnp.zeros_like(extra_ref)
    for seq in range(gtime_ref.shape[0]):
        extra_ref[pl.ds(buckets[core * gtime_ref.shape[0] + seq], 1), :] += gtime_ref[seq : seq + 1, :]
    extra_ref[buckets_in : buckets_in + 1, :] = ggain_a_ref[...]
    extra_ref[buckets_in + 1 : buckets_in + 2, :] = ggain_m_ref[...]
    extra_ref[buckets_in + 2 : buckets_in + 3, :128] = gscale_ref[...]
    sources = (gpos_ref, gwin_ref, ghead_ref, extra_ref)
    for chunk, pieces in enumerate(plan):
        half, owner = divmod(chunk, batch)
        spot = place(owner, me, orders[half])

        def write(ref):
            for panel in range(panels):
                base = panel * each
                filled = 0
                for source, first, at, size in pieces:
                    ref[spot, base + at : base + at + size, :] = sources[source][
                        first : first + size, panel * 128 : (panel + 1) * 128
                    ].astype(ref.dtype)
                    filled = at + size
                if filled < each:
                    ref[spot, base + filled : base + each, :] = jnp.zeros(
                        (each - filled, 128), ref.dtype
                    )

        @pl.when(core == half)
        def _():
            write(keep_ref)

        @pl.when(core != half)
        def _():
            write(send_ref)


    grows = grows_ref[...]
    per = min(4, batch)
    below = slice(panels * each, None)

    def gather_rows(index, _):
        start = index * per * 2 * span
        row = lax.broadcasted_iota(jnp.int32, (per * 2 * span, ids_ref.shape[1]), 0) + start
        one = jnp.where(row == ids_ref[...], 1.0, 0.0).astype(BF)
        sums = dot(one, grows)
        for owner in range(per):
            for half in range(2):
                part = sums[(owner * 2 + half) * span : (owner * 2 + half + 1) * span, :]
                spot = place(index * per + owner, me, orders[half])

                @pl.when(core == half)
                def _():
                    keep_ref[spot, below, :] = part

                @pl.when(core != half)
                def _():
                    send_ref[spot, below, :] = part.astype(BF)

        return 0

    lax.fori_loop(0, batch // per, gather_rows, 0)


def small_rows(length, width, bucket_count):
    return [length, width, width, -(-(bucket_count + 3) // 16) * 16]


def pack(
    where, buckets, gpos, gwin, ghead, gtime, ggain_a, ggain_m, gscale, ids, grows, batch, span,
    bucket_count,
):
    model, width = gpos.shape[1], gwin.shape[0]
    rows = small_rows(gpos.shape[0], width, bucket_count)
    each, plan = small_plan(rows, 2 * batch)
    shape = (batch, each * (model // 128) + span, 128)
    arrays = [gpos, gwin, ghead, gtime, ggain_a, ggain_m, gscale, ids, grows]
    return launch(
        functools.partial(
            pack_kernel, each=each, plan=plan, orders=bit_orders(batch), buckets_in=bucket_count,
            span=span,
        ),
        arrays,
        [whole(array.shape) for array in arrays],
        [whole(shape)] * 2,
        [jax.ShapeDtypeStruct(shape, F32), jax.ShapeDtypeStruct(shape, BF)],
        (1,),
        "pack_small",
        cost(12), limit=34 * 2**20,
        prefetch=[where, buckets],
        scratch=[pltpu.VMEM((rows[3], model), F32)],
    )


def unpack_kernel(
    where, own_ref, other_ref, mine_ref, table_ref, scal_ref,
    pos_ref, win_ref, head_ref, time_ref, gain_a_ref, gain_m_ref, gtable_ref, turned_ref, extra_ref,
    *, each, plan, orders, vocab,
):
    me, core = where[0], where[1]
    batch = own_ref.shape[0]
    panels = pos_ref.shape[1] // 128
    outs = (pos_ref, win_ref, turned_ref, extra_ref)
    for chunk, pieces in enumerate(plan):
        half, owner = divmod(chunk, batch)
        spot = place(owner, me, orders[half])

        def read(ref):
            for panel in range(panels):
                for source, first, at, size in pieces:
                    base = panel * each + at
                    outs[source][first : first + size, panel * 128 : (panel + 1) * 128] = ref[
                        spot, base : base + size, :
                    ].astype(F32)

        if pieces:

            @pl.when(core == half)
            def _():
                read(own_ref)

            @pl.when(core != half)
            def _():
                read(other_ref)

    head_ref[...] = turned_ref[...].T
    count, width = time_ref.shape[0], table_ref.shape[1]
    time_ref[...] = extra_ref[:count, :]
    gain_a_ref[...] = extra_ref[count, :]
    gain_m_ref[...] = extra_ref[count + 1, :]
    scale = jnp.sum(extra_ref[count + 2 : count + 3, :128], axis=1, keepdims=True)
    mean_norm = scal_ref[0:1, 4:5]
    grad_mean = -math.sqrt(width) / (mean_norm * mean_norm) * scale
    table = table_ref[...].astype(F32)
    norms = jnp.sqrt(jnp.sum(table * table, axis=1, keepdims=True) + 1e-06)
    gtable_ref[...] = mine_ref[: table.shape[0], :] + grad_mean / vocab * table / norms


def unpack(where, own, other, mine, table, scal, length, model, bucket_count, vocab):
    batch = own.shape[0]
    width = table.shape[1]
    rows = small_rows(length, width, bucket_count)
    each, plan = small_plan(rows, 2 * batch)
    shapes = [
        (length, model), (width, model), (model, width), (bucket_count, model), (model,), (model,),
        table.shape,
    ]
    arrays = [own, other, mine, table, scal]
    return launch(
        functools.partial(unpack_kernel, each=each, plan=plan, orders=bit_orders(batch), vocab=vocab),
        arrays,
        [whole(array.shape) for array in arrays],
        [whole(shape) for shape in shapes],
        [jax.ShapeDtypeStruct(shape, F32) for shape in shapes],
        (1,),
        "unpack_small",
        cost(5), limit=24 * 2**20,
        prefetch=[where],
        scratch=[pltpu.VMEM((width, model), F32), pltpu.VMEM((rows[3], model), F32)],
    )


def local(
    word_ids, buckets, noise, table, w_in, time_table, pos_table, gain_attn, w_qkv, w_out,
    gain_mlp, w_up, w_down, w_head,
):
    ORDER.clear()
    seq_rows, half_len = word_ids.shape
    table_span, embed_width = table.shape
    model = w_qkv.shape[0]
    bucket_count = time_table.shape[0]
    batch, cores = lax.axis_size("batch"), lax.axis_size("seq")
    devices = batch * cores
    vocab = table_span * devices
    length = half_len * cores
    seqs = seq_rows // cores
    tokens = seqs * length
    me = lax.axis_index("batch").astype(jnp.int32)
    core = lax.axis_index("seq").astype(jnp.int32)
    where = jnp.stack([me, core])

    def regroup(array):
        own = lax.dynamic_slice_in_dim(array, core * seqs, seqs, 0)
        other = swap(lax.dynamic_slice_in_dim(array, (1 - core) * seqs, seqs, 0))
        return jnp.concatenate(
            [jnp.where(core == 0, own, other), jnp.where(core == 0, other, own)], axis=1
        )

    bucket_hot = (buckets[:, None] == jnp.arange(bucket_count, dtype=jnp.int32)[None, :]).astype(F32)
    span = -(-(table_span + 1) // 16) * 16
    behind = jnp.pad(
        jnp.sum(bucket_hot, axis=0).astype(BF)[None, :],
        ((0, span - table_span - 1), (0, embed_width - bucket_count)),
    )
    own_table, other_table = Gather(jnp.concatenate([table, behind], axis=0), batch).finish(True)
    word_list = regroup(word_ids)
    device = lax.div(word_list, table_span)
    row_in = word_list - device * table_span
    owner, its_core = lax.div(device, cores), lax.rem(device, cores)
    orders = bit_orders(batch)
    spot = jnp.where(its_core == 0, place(owner, me, orders[0]), place(owner, me, orders[1]))
    spot = jnp.where(its_core == core, spot, spot + batch)
    ids = (spot * span + row_in).reshape(1, tokens)
    home = (device * span + row_in).reshape(1, tokens)
    noise_rows = regroup(noise).reshape(tokens, embed_width)

    word, noisy, stream, lefts, packed, scal = embed(
        buckets, ids, own_table, other_table, noise_rows, w_in, time_table, pos_table, gain_attn,
        w_qkv, table_span, where,
    )
    lefts, probs, inv = attend(packed, length, lefts)
    mid, mlp, act, slope, ours, theirs, gpred, branch, ghead = forward(
        where, scal, lefts, stream, word, w_out, gain_mlp, w_up, w_down, w_head, length
    )
    pairs = tokens // length * (packed.shape[1] // (6 * HEAD))
    inner = w_up.shape[1]

    def attend_part(first, last, grads):
        return attend_back(packed, gmixed, lefts, inv, probs, length, first, last - first, grads)

    (down,) = outer(where, branch[None], act[None], batch, 512, by_device=True)
    down_sum = lax.psum_scatter(
        down.reshape(devices, *down.shape[2:]), ("batch", "seq"), scatter_dimension=0, tiled=False
    )
    upin, gmid, grads, gmixed, ggain_m = back(
        mid, slope, gpred, branch, w_out, gain_mlp, w_up, w_down, w_head
    )
    sizes = [0, pairs // 3, pairs * 2 // 3, pairs]
    up = Sum(*outer(where, mlp[None], upin[None], batch, 512))
    for part in range(3):
        grads = attend_part(sizes[part], sizes[part + 1], grads)
        up.fold()
    attn = Sum(*outer(where, lefts, grads, batch))
    up.fold(micros=25)
    attn.fold()
    mlp_all = Gather(up.finish_with(down_sum), batch)
    gpos, gtime, ggain_a, gwin, grows, gscale = input_back(
        scal, gmid, grads, stream, noisy, word, gpred, gain_attn, w_qkv, w_in, length
    )
    attn.fold()
    mlp_all.join()
    small = Sum(
        *pack(
            where, buckets, gpos, gwin, ghead, gtime, ggain_a, ggain_m, gscale, home, grows, batch,
            span, bucket_count,
        )
    )
    attn.fold()
    mlp_all.join(micros=25)
    small.fold(F32)
    output = mend(where, ours, swap(theirs))
    small.fold(F32)
    attn.fold()
    small.fold(F32)
    attn_all = Gather(attn.finish(), batch)
    mlp_all.join()
    small.fold(F32)
    attn_all.join()
    mine = small.finish(F32)
    cut = mine.shape[0] - span
    small_all = Gather(mine[:cut].astype(BF), batch)
    attn_all.join()
    small_all.join()
    small_all.join()
    attn_all.join()
    mlp_own, mlp_other = mlp_all.finish()
    small_all.join()
    (grad_up,) = spread_near(where, mlp_own, mlp_other, 1, model, (inner,))
    (grad_down,) = spread_near(where, mlp_own, mlp_other, 0, model, (inner,), True)
    small_all.join(micros=25)
    attn_own, attn_other = attn_all.finish()
    small_own, small_other = small_all.finish()
    grad_qkv, grad_out = spread_near(
        where, attn_own[:, None], attn_other[:, None], 0, model, (3 * model, model)
    )
    pos_sum, win_sum, head_sum, time_sum, gain_a_sum, gain_m_sum, grad_table = unpack(
        where, small_own, small_other, mine[cut:], table, scal, length, model, bucket_count, vocab
    )
    return (
        output,
        grad_table,
        win_sum,
        time_sum,
        pos_sum,
        gain_a_sum,
        grad_qkv,
        grad_out,
        gain_m_sum,
        grad_up,
        grad_down,
        head_sum,
        scal[0, 4],
    )


def solution(mesh):
    rows = P(("batch", "seq"), None)
    in_specs = (P("batch", "seq"), P("batch"), P("batch", "seq", None), rows) + (P(),) * 10
    out_specs = (P("batch", "seq", None), rows) + (P(),) * 11
    return jax.shard_map(local, mesh=mesh, in_specs=in_specs, out_specs=out_specs, check_vma=False)
```
